32 devices in a mesh: wide: 16 (over z, y, core), narrow: 2 (over x).
Axes of the slice: x: 2, y: 2, z: 4, core: 2. Of those that a mesh axis runs over, the one named last changes fastest.
Arguments:
- layer_input: bfloat16 [2048, 119, 192], P(('wide', 'narrow')), may hold values from -6 to 6
- mask: int32 [2048, 119], P(('wide', 'narrow')), may hold values 0 or 1
- dout: bfloat16 [2048, 119, 192], P(('wide', 'narrow')), may hold values from -6 to 6
- attn_w: float32 [4, 192, 192], P(None, 'wide'), may hold values from -0.57735027 to 0.57735027
- ffn_in: float32 [192, 512], P('wide'), may hold values from -0.4375 to 0.4375
- ffn_out: float32 [256, 192], P('wide'), may hold values from -0.375 to 0.375
- vec: float32 [2048], P('wide'), may hold values from -1.2 to 1.6
- m_attn: float32 [4, 192, 192], P(None, 'wide'), may hold values from -112 to 112
- v_attn: float32 [4, 192, 192], P(None, 'wide'), may hold values from 24.3712 to 97.4848
- m_in: float32 [192, 512], P('wide'), may hold values from -160 to 160
- v_in: float32 [192, 512], P('wide'), may hold values from 60.928 to 243.712
- m_out: float32 [256, 192], P('wide'), may hold values from -192 to 192
- v_out: float32 [256, 192], P('wide'), may hold values from 87.73632 to 350.94528
- m_vec: float32 [2048], P('wide'), may hold values from -224 to 224
- v_vec: float32 [2048], P('wide'), may hold values from 119.41888 to 477.6755
Outputs:
- layer_output: bfloat16 [2048, 119, 192], P(('wide', 'narrow'))
- dx: bfloat16 [2048, 119, 192], P(('wide', 'narrow'))
- new_attn_w: float32 [4, 192, 192], P(None, 'wide')
- new_m_attn: float32 [4, 192, 192], P(None, 'wide')
- new_v_attn: float32 [4, 192, 192], P(None, 'wide')
- new_ffn_in: float32 [192, 512], P('wide')
- new_m_in: float32 [192, 512], P('wide')
- new_v_in: float32 [192, 512], P('wide')
- new_ffn_out: float32 [256, 192], P('wide')
- new_m_out: float32 [256, 192], P('wide')
- new_v_out: float32 [256, 192], P('wide')
- new_vec: float32 [2048], P('wide')
- new_m_vec: float32 [2048], P('wide')
- new_v_vec: float32 [2048], P('wide')
The draws below stay inside these ranges and needn't reach their ends.
All inputs are finite; a program needn't handle non-finite values. No bound on the sum of `mask` on one device may be relied on, other than what follows from the above.
Results may differ from the reference program's by a relative error of at most 0.012.
The reference program's roundings to bfloat16 on the way count: a program that leaves them out, or rounds other values in their place, can miss the bound.
Values may be sent and summed in bfloat16 or wider, within the bound.
A program may use at most 256 MiB of HBM per device.

```python
import math
import jax
import jax.numpy as jnp
from jax import lax

D = 192
H = 8
FH = 256
STEP = 10
L = 119
VLEN = 2048
SAMP = 2048
TOKENS = 243712


def draw_attn_w(key, part):
    scales = jnp.array([D ** (-0.5), D ** (-0.5), D ** (-0.5), max(D // 4, 1) ** (-0.5)], jnp.float32).reshape(4, 1, 1)
    base = jax.random.truncated_normal(key, -4.0, 4.0, (4, D, D), jnp.float32)
    return base * scales


def draw_vec(key, part):
    key_gain = jax.random.fold_in(key, 11)
    key_bias = jax.random.fold_in(key, 12)
    count = 6 * D + 2 * FH
    gains = 1.0 + 0.15 * jax.random.truncated_normal(key_gain, -4.0, 4.0, (2, D), jnp.float32)
    biases = 0.3 * jax.random.truncated_normal(key_bias, -4.0, 4.0, (count,), jnp.float32)
    return jnp.concatenate([gains[0], biases[:4 * D], gains[1], biases[4 * D:]])


def touch_ends(entries, rng, least, largest):
    shape = entries.shape
    spot = [jax.random.randint(jax.random.fold_in(rng, axis), (), 0, shape[axis]) for axis in range(len(shape))]
    entries = entries.at[tuple(spot)].set(least)
    longest = shape.index(max(shape))
    spot[longest] = (spot[longest] + 1) % shape[longest]
    return entries.at[tuple(spot)].set(largest)


def level_of(own_key, dims, split, smallest, top_value):
    level, own = 1.0, jax.random.fold_in(own_key, 6)
    for dim, shards_of in split:
        draws = jnp.exp(jax.random.uniform(jax.random.fold_in(own, dim), (shards_of,), jnp.float32, smallest / len(split), top_value / len(split)))
        level = level * jnp.repeat(draws, dims[dim] // shards_of).reshape([-1 if axis == dim else 1 for axis in range(len(dims))])
    return level


def normal_values(key, dims, scale, limit, cuts=(), kind=jnp.bfloat16):
    gain = level_of(key, dims, cuts, -0.22, 0.18) if cuts else 1.0
    values = jax.random.normal(key, dims, jnp.float32) * scale * gain
    return jnp.minimum(jnp.maximum(values, -limit), limit).astype(kind)


def setup_inputs(seed: int = 0) -> dict:
    keys = jax.random.split(jax.random.key(seed), 16)
    layer_input = normal_values(keys[0], (SAMP, L, D), 1.0, 6.0, ((0, 32),))
    mask = touch_ends((jax.random.randint(keys[1], (SAMP, L), 0, 4) < 3).astype(jnp.int32), jax.random.fold_in(keys[1], 1), 0, 1)
    dout = normal_values(keys[2], (SAMP, L, D), 1.0, 6.0, ((0, 32),))
    attn_w = draw_attn_w(jax.random.fold_in(keys[15], 71), 0)
    ffn_in = normal_values(keys[4], (D, 2 * FH), D ** -0.5, 0.4375, ((0, 16),), jnp.float32)
    ffn_out = normal_values(keys[5], (FH, D), FH ** -0.5, 0.375, ((0, 16),), jnp.float32)
    vec = draw_vec(jax.random.fold_in(keys[15], 71), 0)
    m_attn = normal_values(keys[7], (4, D, D), (0.035 * TOKENS ** 0.5), 112.0, ((1, 16),), jnp.float32)
    v_attn = jnp.clip(jnp.exp(math.log(97.4848) - 1.3862944 * jax.random.uniform(keys[8], (4, D, D), jnp.float32) ** level_of(keys[8], (4, D, D), ((1, 16),), -0.2, 0.2)), 24.3712, 97.4848)
    m_in = normal_values(keys[9], (D, 2 * FH), (0.055 * TOKENS ** 0.5), 160.0, ((0, 16),), jnp.float32)
    v_in = jnp.clip(jnp.exp(math.log(243.712) - 1.3862944 * jax.random.uniform(keys[10], (D, 2 * FH), jnp.float32) ** level_of(keys[10], (D, 2 * FH), ((0, 16),), -0.2, 0.2)), 60.928, 243.712)
    m_out = normal_values(keys[11], (FH, D), (0.066 * TOKENS ** 0.5), 192.0, ((0, 16),), jnp.float32)
    v_out = jnp.clip(jnp.exp(math.log(350.94528) - 1.3862944 * jax.random.uniform(keys[12], (FH, D), jnp.float32) ** level_of(keys[12], (FH, D), ((0, 16),), -0.2, 0.2)), 87.73632, 350.94528)
    m_vec = normal_values(keys[13], (VLEN,), (0.077 * TOKENS ** 0.5), 224.0, ((0, 16),), jnp.float32)
    v_vec = jnp.clip(jnp.exp(math.log(477.6755) - 1.3862944 * jax.random.uniform(keys[14], (VLEN,), jnp.float32) ** level_of(keys[14], (VLEN,), ((0, 16),), -0.2, 0.2)), 119.41888, 477.6755)
    return {"layer_input": layer_input, "mask": mask, "dout": dout, "attn_w": attn_w, "ffn_in": ffn_in, "ffn_out": ffn_out, "vec": vec, "m_attn": m_attn, "v_attn": v_attn, "m_in": m_in, "v_in": v_in, "m_out": m_out, "v_out": v_out, "m_vec": m_vec, "v_vec": v_vec}


@jax.custom_vjp
def low(v):
    return lax.optimization_barrier(v.astype(jnp.bfloat16)).astype(jnp.float32)

@jax.custom_vjp
def low_back(v):
    return v

def low_keep(v):
    return (low(v), None)

def low_pass(kept, grad):
    return (grad,)

def back_keep(v):
    return (v, None)

def back_low(kept, grad):
    return (low(grad),)
low.defvjp(low_keep, low_pass)
low_back.defvjp(back_keep, back_low)

def layer_norm(value):
    center = value - lax.optimization_barrier(jnp.mean(value, -1, keepdims=True))
    return center * lax.rsqrt(lax.optimization_barrier(jnp.mean(center * center, -1, keepdims=True)) + 1e-05)

def project(left_term, right_term):
    return jnp.einsum('qab,bm->qam', left_term, right_term, precision=lax.Precision.HIGHEST)

def forward(xb, valid, attn_w, ffn_in, ffn_out, vec):
    highest = lax.Precision.HIGHEST
    weights = low(attn_w)
    w_in = low(ffn_in)
    w_out = low(ffn_out)
    vector = low(vec)
    pieces = [vector[i * D:(i + 1) * D] for i in range(8)]
    first_norm_gain, first_norm_bias, bias_q, bias_v, bias_o, second_norm_gain, second_norm_bias, bias_c2 = pieces
    bias_c1 = vector[8 * D:8 * D + 2 * FH]
    samples = xb.shape[0]
    head_size = D // H
    first_normed_rows = low(layer_norm(xb) * first_norm_gain + first_norm_bias)
    query = low(low_back(project(first_normed_rows, weights[0]) + bias_q)).reshape(samples, L, H, head_size)
    keyed = low(low_back(project(first_normed_rows, weights[1]))).reshape(samples, L, H, head_size)
    valued = low(low_back(project(first_normed_rows, weights[2]) + bias_v)).reshape(samples, L, H, head_size)
    scores = low_back(jnp.einsum('slhe,smhe->shlm', query, keyed, precision=highest) * float(head_size) ** (-0.5))
    scores = jnp.where(valid[:, None, None, :], scores, -1e+30)
    probs = jax.nn.softmax(scores, axis=-1)
    mixed = jnp.einsum('shlm,smhe->slhe', low(probs), valued, precision=highest)
    mixed = low(low_back(mixed)).reshape(samples, L, D)
    branch = low_back(project(mixed, weights[3]) + bias_o)
    first_branch = xb + branch
    second_normed_rows = low(layer_norm(first_branch) * second_norm_gain + second_norm_bias)
    gated = low_back(project(second_normed_rows, w_in) + bias_c1)
    hidden = low(gated[..., :FH] * jax.nn.silu(gated[..., FH:]))
    return first_branch + project(hidden, w_out) + bias_c2

def adamw(weight, first_m, second_m, grad, decay):
    new_m = 0.9 * first_m + 0.1 * grad
    new_v = 0.999 * second_m + 0.001 * grad * grad
    ratio = new_m / (1.0 - 0.9 ** STEP) / (jnp.sqrt(new_v / (1.0 - 0.999 ** STEP)) + 1e-08)
    return (weight - 0.1 * (ratio + decay * weight), new_m, new_v)

def reference(layer_input, mask, dout, attn_w, ffn_in, ffn_out, vec, m_attn, v_attn, m_in, v_in, m_out, v_out, m_vec, v_vec):
    block = math.gcd(SAMP, 32)
    count = SAMP // block
    valid = (mask != 0) | (jnp.arange(L, dtype=jnp.int32)[None, :] == 0)
    x_blocks = layer_input.astype(jnp.float32).reshape(count, block, L, D)
    v_blocks = valid.reshape(count, block, L)
    d_blocks = dout.astype(jnp.float32).reshape(count, block, L, D)

    def visit(carry, item):
        xb, vb, db = item
        yb, pull = jax.vjp(lambda aa, bb, cc, dd, ee: forward(aa, vb, bb, cc, dd, ee), xb, attn_w, ffn_in, ffn_out, vec)
        gx, ga, gi, go, gv = pull(db)
        carry = (carry[0] + ga, carry[1] + gi, carry[2] + go, carry[3] + gv)
        return (carry, (yb.astype(jnp.bfloat16), gx.astype(jnp.bfloat16)))
    start = (jnp.zeros_like(attn_w), jnp.zeros_like(ffn_in), jnp.zeros_like(ffn_out), jnp.zeros_like(vec))
    grads, (ys, gxs) = lax.scan(visit, start, (x_blocks, v_blocks, d_blocks))
    layer_output = ys.reshape(SAMP, L, D)
    dx = gxs.reshape(SAMP, L, D)
    wa, ma, va = adamw(attn_w, m_attn, v_attn, grads[0], 0.01)
    wi, mi, vi = adamw(ffn_in, m_in, v_in, grads[1], 0.01)
    wo, mo, vo = adamw(ffn_out, m_out, v_out, grads[2], 0.01)
    wv, mv, vv = adamw(vec, m_vec, v_vec, grads[3], 0.0)
    return (layer_output, dx, wa, ma, va, wi, mi, vi, wo, mo, vo, wv, mv, vv)
```

```python
import functools
import jax
import jax.numpy as jnp
from jax import lax
from jax.experimental import pallas as pl
from jax.experimental.pallas import tpu as pltpu
from jax.sharding import PartitionSpec as P

H = 8
FH = 256
STEP = 10
LANES = 128
F32 = jnp.float32
BF16 = jnp.bfloat16
NN = (((1,), (0,)), ((), ()))
NT = (((1,), (1,)), ((), ()))


def mm(a, b, dims=NN):
    return lax.dot_general(a, b, dims, preferred_element_type=F32)


def layer_kernel(
    group,
    x_ref, mask_ref, g_ref, wqkv_ref, wo_ref, w1_ref, w2_ref, vec_ref,
    y_ref, dx_ref, gqkv_ref, go_ref, g1_ref, g2_ref, gln_ref,
    wqkvt, wot, w1t, w2t, cols, n1a, n2a, oa, ha, e_s, ln_acc,
):
    step = pl.program_id(0)
    length = x_ref.shape[2]
    width = x_ref.shape[1]
    head = width // H
    tokens = group * LANES
    factor = float(head) ** (-0.5)
    log2e = 1.4426950408889634

    @pl.when(step == 0)
    def _():
        def aug(w, bias):
            rows = lax.broadcasted_iota(jnp.int32, (64, w.shape[1]), 0)
            tail = jnp.where(rows == 0, jnp.broadcast_to(bias, (64, w.shape[1])), 0.0)
            return jnp.concatenate([w.astype(F32), tail], axis=0).T.astype(BF16)

        zero_row = jnp.zeros((1, width), F32)
        v = vec_ref[...]
        piece = lambda i: v[:, i * width : (i + 1) * width]
        bias_qkv = jnp.concatenate([piece(2), zero_row, piece(3)], axis=1)
        wqkvt[...] = aug(wqkv_ref[...], bias_qkv)
        wot[...] = aug(wo_ref[...], piece(4))
        w1t[...] = aug(w1_ref[...], v[:, 8 * width : 8 * width + 2 * FH])
        w2t[...] = w2_ref[...].astype(F32).T.astype(BF16)
        for j, i in enumerate((0, 1, 5, 6, 7)):
            cols[j] = jnp.broadcast_to(piece(i), (LANES, width)).T
        rows = lax.broadcasted_iota(jnp.int32, (64, tokens), 0)
        one = jnp.where(rows == 0, 1.0, 0.0).astype(BF16)
        n1a[width:, :] = one
        n2a[width:, :] = one
        oa[width:, :] = one
        ha[FH:, :] = one[:16]
        gqkv_ref[...] = jnp.zeros_like(gqkv_ref)
        go_ref[...] = jnp.zeros_like(go_ref)
        g1_ref[...] = jnp.zeros_like(g1_ref)
        g2_ref[...] = jnp.zeros_like(g2_ref)
        ln_acc[...] = jnp.zeros_like(ln_acc)

    def wide(ref, g):
        t = ref[g]
        return jnp.concatenate([t, jnp.zeros((width, LANES - length), t.dtype)], axis=1)

    def tile(col):
        return jnp.concatenate([col] * group, axis=1) if group > 1 else col

    def norm(value):
        center = value - jnp.sum(value, 0, keepdims=True) * (1.0 / width)
        rstd = lax.rsqrt(jnp.sum(center * center, 0, keepdims=True) * (1.0 / width) + 1e-05)
        return center * rstd, rstd

    def norm_back(dn, xhat, rstd, gain, which):
        prod = dn * xhat
        a0, a1 = ln_acc[2 * which], ln_acc[2 * which + 1]
        for g in range(group):
            sl = slice(g * LANES, (g + 1) * LANES)
            a0 = a0 + prod[:, sl]
            a1 = a1 + dn[:, sl]
        ln_acc[2 * which] = a0
        ln_acc[2 * which + 1] = a1
        t = dn * gain
        m1 = jnp.sum(t, 0, keepdims=True) * (1.0 / width)
        m2 = jnp.sum(t * xhat, 0, keepdims=True) * (1.0 / width)
        return rstd * (t - m1 - xhat * m2)

    gain1, bias1, gain2, bias2, bias_c2 = (tile(cols[j]) for j in range(5))

    x = jnp.concatenate([wide(x_ref, g) for g in range(group)], axis=1).astype(F32)
    xhat1, rstd1 = norm(x)
    n1a[:width, :] = (xhat1 * gain1 + bias1).astype(BF16)
    qkv = mm(wqkvt[...], n1a[...])

    sub = lax.broadcasted_iota(jnp.int32, (8, LANES), 0)
    lane = lax.broadcasted_iota(jnp.int32, (8, LANES), 1)
    tile_q = jnp.where(sub == 0, 1.0, 0.0)
    tile_v = jnp.where(sub < 2, 1.0, 0.0)
    zeros = jnp.zeros((32, LANES), BF16)

    def padded(rows, tail):
        return jnp.concatenate([rows, tail], axis=0).astype(BF16)

    def pair_diag(a, b):
        return jnp.concatenate(
            [jnp.concatenate([a, zeros], axis=1), jnp.concatenate([zeros, b], axis=1)], axis=0
        )

    kept = []
    mixed = []
    for g in range(group):
        sl = slice(g * LANES, (g + 1) * LANES)
        m = mask_ref[pl.ds(step * group + g, 1), :]
        m = jnp.concatenate([m, jnp.zeros((1, LANES - length), jnp.int32)], axis=1)
        m8 = jnp.broadcast_to(m, (8, LANES))
        ok = (m8 != 0) | (lane == 0)
        tile_k = jnp.where((sub == 0) & jnp.logical_not(ok), -1e30, 0.0)
        mixed_rows = []
        for p in range(H // 2):
            qs, ks, vs = [], [], []
            for h in (2 * p, 2 * p + 1):
                r = slice(h * head, (h + 1) * head)
                qs.append(padded(qkv[r.start : r.stop, sl], tile_q))
                ks.append(padded(qkv[width + r.start : width + r.stop, sl], tile_k))
                vs.append(padded(qkv[2 * width + r.start : 2 * width + r.stop, sl], tile_v))
            qd = pair_diag(*qs)
            kp = jnp.concatenate(ks, axis=0)
            vp = jnp.concatenate(vs, axis=0)
            s = mm(kp.T, qd)
            top = jnp.max(s, 0, keepdims=True)
            e = jnp.exp2((s - top) * (factor * log2e)).astype(BF16)
            e_s[g, p] = e
            num = mm(vp, e)
            for j in range(2):
                part = num[32 * j : 32 * j + 32, j * LANES : (j + 1) * LANES]
                inv = 1.0 / part[head : head + 1]
                o = part[:head] * inv
                mixed_rows.append(o)
                kept.append((inv, o))
            kept[-1] = kept[-1] + (qd, kp, vp)
        mixed.append(jnp.concatenate(mixed_rows, axis=0))
    oa[:width, :] = jnp.concatenate(mixed, axis=1).astype(BF16)
    x1 = x + mm(wot[...], oa[...])
    xhat2, rstd2 = norm(x1)
    n2a[:width, :] = (xhat2 * gain2 + bias2).astype(BF16)
    z = mm(w1t[...], n2a[...])
    part_a, part_b = z[:FH], z[FH:]
    sigm = 1.0 / (1.0 + jnp.exp2(part_b * -log2e))
    silu = part_b * sigm
    ha[:FH, :] = (part_a * silu).astype(BF16)
    y = (x1 + mm(w2t[...], ha[:FH, :]) + bias_c2).astype(BF16)
    for g in range(group):
        y_ref[g] = y[:, g * LANES : g * LANES + length]

    gt = jnp.concatenate([wide(g_ref, g) for g in range(group)], axis=1)
    g2_ref[...] += mm(ha[...], gt, NT)
    dh = mm(w2_ref[...], gt)
    da = dh * silu
    db = dh * part_a * sigm * (1.0 + part_b * (1.0 - sigm))
    dz = jnp.concatenate([da, db], axis=0).astype(BF16)
    g1_ref[...] += mm(n2a[:208, :], dz, NT)
    dn2 = mm(w1_ref[...], dz)
    dx1 = gt.astype(F32) + norm_back(dn2, xhat2, rstd2, gain2, 1)
    da1 = dx1.astype(BF16)
    go_ref[...] += mm(oa[:208, :], da1, NT)
    do = mm(wo_ref[...], da1).astype(BF16).astype(F32)

    parts = []
    for g in range(group):
        sl = slice(g * LANES, (g + 1) * LANES)
        dqs, dks, dvs = [], [], []
        for p in range(H // 2):
            ds_ = []
            for j in range(2):
                h = 2 * p + j
                inv, o = kept[g * H + h][:2]
                d = do[h * head : (h + 1) * head, sl]
                low = jnp.sum(d * o, 0, keepdims=True) * -inv
                hi = low.astype(BF16).astype(F32)
                lo = low - hi
                tail = jnp.where(sub == 0, hi, jnp.where(sub == 1, lo, 0.0))
                ds_.append(padded(d * inv, tail))
            qd, kp, vp = kept[g * H + 2 * p + 1][2:]
            dd = pair_diag(*ds_)
            e = e_s[g, p]
            dpd = mm(vp.T, dd)
            dsc = (e.astype(F32) * dpd).astype(BF16)
            dv = mm(dd, e, NT)
            dq = mm(kp, dsc)
            dk = mm(qd, dsc, NT)
            for j in range(2):
                dqs.append(dq[32 * j : 32 * j + head, j * LANES : (j + 1) * LANES] * factor)
                dks.append(dk[32 * j : 32 * j + head] * factor)
                dvs.append(dv[32 * j : 32 * j + head])
        parts.append(jnp.concatenate(dqs + dks + dvs, axis=0))
    dqkv = jnp.concatenate(parts, axis=1).astype(BF16)
    gqkv_ref[...] += mm(n1a[:208, :], dqkv, NT)
    dn1 = mm(wqkv_ref[...], dqkv)
    dx = (dx1 + norm_back(dn1, xhat1, rstd1, gain1, 0)).astype(BF16)
    for g in range(group):
        dx_ref[g] = dx[:, g * LANES : g * LANES + length]

    @pl.when(step == pl.num_programs(0) - 1)
    def _():
        rows = [jnp.sum(ln_acc[i].T, 0, keepdims=True) for i in range(4)]
        gln_ref[...] = jnp.concatenate(rows + [jnp.zeros((4, width), F32)], axis=0)


def run_layer(x, mask, dout, wqkv, wo, w1, w2, vec, group=2):
    samples, width, length = x.shape
    tokens = group * LANES
    whole = lambda a: pl.BlockSpec(a.shape, lambda i: (0,) * a.ndim)
    per = pl.BlockSpec((group, width, length), lambda i: (i, 0, 0))
    const = lambda shape: pl.BlockSpec(shape, lambda i: (0,) * len(shape))
    shapes = [(208, 3 * width), (208, width), (208, 2 * FH), (272, width), (8, width)]
    return pl.pallas_call(
        functools.partial(layer_kernel, group),
        grid=(samples // group,),
        in_specs=[per, whole(mask), per, whole(wqkv), whole(wo), whole(w1), whole(w2), whole(vec)],
        out_specs=[per, per] + [const(s) for s in shapes],
        out_shape=[jax.ShapeDtypeStruct(x.shape, BF16)] * 2
        + [jax.ShapeDtypeStruct(s, F32) for s in shapes],
        scratch_shapes=[
            pltpu.VMEM((3 * width, 256), BF16),
            pltpu.VMEM((width, 256), BF16),
            pltpu.VMEM((2 * FH, 256), BF16),
            pltpu.VMEM((width, FH), BF16),
            pltpu.VMEM((5, width, LANES), F32),
            pltpu.VMEM((256, tokens), BF16),
            pltpu.VMEM((256, tokens), BF16),
            pltpu.VMEM((256, tokens), BF16),
            pltpu.VMEM((272, tokens), BF16),
            pltpu.VMEM((group, H // 2, LANES, 2 * LANES), BF16),
            pltpu.VMEM((4, width, LANES), F32),
        ],
        compiler_params=pltpu.CompilerParams(vmem_limit_bytes=60 * 1024 * 1024),
        name="layer",
    )(x, mask, dout, wqkv, wo, w1, w2, vec)


def adamw(weight, first_m, second_m, grad, decay):
    new_m = 0.9 * first_m + 0.1 * grad
    new_v = 0.999 * second_m + 0.001 * grad * grad
    ratio = new_m / (1.0 - 0.9**STEP) / (jnp.sqrt(new_v / (1.0 - 0.999**STEP)) + 1e-08)
    return (weight - 0.1 * (ratio + decay * weight), new_m, new_v)


def on_device(layer_input, mask, dout, attn_w, ffn_in, ffn_out, vec,
              m_attn, v_attn, m_in, v_in, m_out, v_out, m_vec, v_vec):
    width = layer_input.shape[2]
    n = lax.axis_size("wide")
    shard = (attn_w, ffn_in, ffn_out, vec)
    sizes = [a.size for a in shard]
    flat = jnp.concatenate([a.astype(BF16).reshape(-1) for a in shard])
    full = lax.all_gather(flat, "wide", axis=0, tiled=False)
    ends = [sum(sizes[:i]) for i in range(5)]
    cut = lambda i: full[:, ends[i] : ends[i + 1]]
    r = attn_w.shape[1]
    weights = cut(0).reshape(n, 4, r, width).transpose(1, 0, 2, 3).reshape(4, width, width)
    w1 = cut(1).reshape(width, 2 * FH)
    w2 = cut(2).reshape(FH, width)
    vector = cut(3).reshape(1, -1).astype(F32)
    wqkv = jnp.concatenate([weights[0], weights[1], weights[2]], axis=1)
    y, dx, gqkv, go, g1, g2, gln = run_layer(
        layer_input.transpose(0, 2, 1), mask, dout.transpose(0, 2, 1), wqkv, weights[3], w1, w2, vector
    )
    grad_attn = jnp.stack([gqkv[:width, :width], gqkv[:width, width : 2 * width], gqkv[:width, 2 * width :], go[:width]])
    grad_vec = jnp.concatenate([gln[0], gln[1], gqkv[width, :width], gqkv[width, 2 * width :], go[width],
                                gln[2], gln[3], g2[FH], g1[width]])
    parts = [
        grad_attn.reshape(4, n, r, width).transpose(1, 0, 2, 3).reshape(n, -1),
        g1[:width].reshape(n, -1),
        g2[:FH].reshape(n, -1),
        grad_vec.reshape(n, -1),
    ]
    packed = lax.psum(jnp.concatenate(parts, axis=1), "narrow")
    mine = lax.psum_scatter(packed, "wide", scatter_dimension=0, tiled=False)
    shares = [mine[ends[i] : ends[i + 1]].reshape(shard[i].shape) for i in range(4)]
    wa, ma, va = adamw(attn_w, m_attn, v_attn, shares[0], 0.01)
    wi, mi, vi = adamw(ffn_in, m_in, v_in, shares[1], 0.01)
    wo, mo, vo = adamw(ffn_out, m_out, v_out, shares[2], 0.01)
    wv, mv, vv = adamw(vec, m_vec, v_vec, shares[3], 0.0)
    return (y.transpose(0, 2, 1), dx.transpose(0, 2, 1), wa, ma, va, wi, mi, vi, wo, mo, vo, wv, mv, vv)


def solution(mesh):
    rows = P(("wide", "narrow"), None, None)
    states = [P(None, "wide", None), P("wide", None), P("wide", None), P("wide")]
    moments = [s for s in states for _ in range(2)]
    results = [s for s in states for _ in range(3)]
    return jax.shard_map(
        on_device,
        mesh=mesh,
        in_specs=tuple([rows, P(("wide", "narrow"), None), rows] + states + moments),
        out_specs=tuple([rows, rows] + results),
        check_vma=False,
    )
```

```python
import functools
import jax
import jax.numpy as jnp
from jax import lax
from jax.experimental import pallas as pl
from jax.experimental.pallas import tpu as pltpu
from jax.sharding import PartitionSpec as P

H = 8
FH = 256
STEP = 10
LANES = 128
GROUP = 2
F32 = jnp.float32
BF16 = jnp.bfloat16
NN = (((1,), (0,)), ((), ()))
NT = (((1,), (1,)), ((), ()))


def mm(a, b, dims=NN):
    return lax.dot_general(a, b, dims, preferred_element_type=F32)


def layer_kernel(
    group,
    x_ref, mask_ref, g_ref, full_ref,
    y_ref, dx_ref, packed_ref,
    big, w2f, vec_s, wqkv_ref, wo_ref, w1_ref, w2_ref,
    wqkvt, wot, w1t, w2t, cols, n1a, n2a, oa, ha, e_s,
    gqkv_ref, go_ref, g1_ref, g2_ref, ln_acc, pack_s,
):
    step = pl.program_id(0)
    length = x_ref.shape[2]
    width = x_ref.shape[1]
    head = width // H
    tokens = group * LANES
    factor = float(head) ** (-0.5)
    log2e = 1.4426950408889634

    @pl.when(step == 0)
    def _():
        shards, block_rows, _ = full_ref.shape
        depth = width // shards
        extra = block_rows - depth
        per_vec = vec_s.shape[1] // shards
        for w in range(shards):
            block = full_ref[w].astype(F32)
            big[w * depth : (w + 1) * depth, :] = block[:depth]
            for j in range(4):
                at = (4 * w + j) * extra
                w2f[at : at + extra, :] = block[depth:, j * width : (j + 1) * width]
            vec_s[:, w * per_vec : (w + 1) * per_vec] = block[depth : depth + 1, 4 * width : 4 * width + per_vec]
        wqkv_ref[...] = big[:, : 3 * width].astype(BF16)
        wo_ref[...] = big[:, 3 * width : 4 * width].astype(BF16)
        w1_ref[...] = big[:, 4 * width :].astype(BF16)
        w2_ref[...] = w2f[...].astype(BF16)

        def aug(w, bias):
            rows = lax.broadcasted_iota(jnp.int32, (64, w.shape[1]), 0)
            tail = jnp.where(rows == 0, jnp.broadcast_to(bias, (64, w.shape[1])), 0.0)
            return jnp.concatenate([w.astype(F32), tail], axis=0).T.astype(BF16)

        zero_row = jnp.zeros((1, width), F32)
        v = vec_s[...]
        piece = lambda i: v[:, i * width : (i + 1) * width]
        bias_qkv = jnp.concatenate([piece(2), zero_row, piece(3)], axis=1)
        wqkvt[...] = aug(wqkv_ref[...], bias_qkv)
        wot[...] = aug(wo_ref[...], piece(4))
        w1t[...] = aug(w1_ref[...], v[:, 8 * width : 8 * width + 2 * FH])
        w2t[...] = w2_ref[...].astype(F32).T.astype(BF16)
        for j, i in enumerate((0, 1, 5, 6, 7)):
            cols[j] = jnp.broadcast_to(piece(i), (LANES, width)).T
        rows = lax.broadcasted_iota(jnp.int32, (64, tokens), 0)
        one = jnp.where(rows == 0, 1.0, 0.0).astype(BF16)
        n1a[width:, :] = one
        n2a[width:, :] = one
        oa[width:, :] = one
        ha[FH:, :] = one[:16]
        gqkv_ref[...] = jnp.zeros_like(gqkv_ref)
        go_ref[...] = jnp.zeros_like(go_ref)
        g1_ref[...] = jnp.zeros_like(g1_ref)
        g2_ref[...] = jnp.zeros_like(g2_ref)
        ln_acc[...] = jnp.zeros_like(ln_acc)

    def wide(ref, g):
        t = ref[g]
        return jnp.concatenate([t, jnp.zeros((width, LANES - length), t.dtype)], axis=1)

    def tile(col):
        return jnp.concatenate([col] * group, axis=1) if group > 1 else col

    def norm(value):
        center = value - jnp.sum(value, 0, keepdims=True) * (1.0 / width)
        rstd = lax.rsqrt(jnp.sum(center * center, 0, keepdims=True) * (1.0 / width) + 1e-05)
        return center * rstd, rstd

    def norm_back(dn, xhat, rstd, gain, which):
        prod = dn * xhat
        a0, a1 = ln_acc[2 * which], ln_acc[2 * which + 1]
        for g in range(group):
            sl = slice(g * LANES, (g + 1) * LANES)
            a0 = a0 + prod[:, sl]
            a1 = a1 + dn[:, sl]
        ln_acc[2 * which] = a0
        ln_acc[2 * which + 1] = a1
        t = dn * gain
        m1 = jnp.sum(t, 0, keepdims=True) * (1.0 / width)
        m2 = jnp.sum(t * xhat, 0, keepdims=True) * (1.0 / width)
        return rstd * (t - m1 - xhat * m2)

    gain1, bias1, gain2, bias2, bias_c2 = (tile(cols[j]) for j in range(5))

    x = jnp.concatenate([wide(x_ref, g) for g in range(group)], axis=1).astype(F32)
    xhat1, rstd1 = norm(x)
    n1a[:width, :] = (xhat1 * gain1 + bias1).astype(BF16)
    qkv = mm(wqkvt[...], n1a[...])

    sub = lax.broadcasted_iota(jnp.int32, (8, LANES), 0)
    lane = lax.broadcasted_iota(jnp.int32, (8, LANES), 1)
    tile_q = jnp.where(sub == 0, 1.0, 0.0)
    tile_v = jnp.where(sub < 2, 1.0, 0.0)
    zeros = jnp.zeros((32, LANES), BF16)

    def padded(rows, tail):
        return jnp.concatenate([rows, tail], axis=0).astype(BF16)

    def pair_diag(a, b):
        return jnp.concatenate(
            [jnp.concatenate([a, zeros], axis=1), jnp.concatenate([zeros, b], axis=1)], axis=0
        )

    kept = []
    mixed = []
    for g in range(group):
        sl = slice(g * LANES, (g + 1) * LANES)
        m = mask_ref[pl.ds(step * group + g, 1), :]
        m = jnp.concatenate([m, jnp.zeros((1, LANES - length), jnp.int32)], axis=1)
        m8 = jnp.broadcast_to(m, (8, LANES))
        ok = (m8 != 0) | (lane == 0)
        tile_k = jnp.where((sub == 0) & jnp.logical_not(ok), -1e30, 0.0)
        mixed_rows = []
        for p in range(H // 2):
            qs, ks, vs = [], [], []
            for h in (2 * p, 2 * p + 1):
                r = slice(h * head, (h + 1) * head)
                qs.append(padded(qkv[r.start : r.stop, sl], tile_q))
                ks.append(padded(qkv[width + r.start : width + r.stop, sl], tile_k))
                vs.append(padded(qkv[2 * width + r.start : 2 * width + r.stop, sl], tile_v))
            qd = pair_diag(*qs)
            kp = jnp.concatenate(ks, axis=0)
            vp = jnp.concatenate(vs, axis=0)
            s = mm(kp.T, qd)
            top = jnp.max(s, 0, keepdims=True)
            e = jnp.exp2((s - top) * (factor * log2e)).astype(BF16)
            e_s[g, p] = e
            num = mm(vp, e)
            for j in range(2):
                part = num[32 * j : 32 * j + 32, j * LANES : (j + 1) * LANES]
                inv = 1.0 / part[head : head + 1]
                o = part[:head] * inv
                mixed_rows.append(o)
                kept.append((inv, o))
            kept[-1] = kept[-1] + (qd, kp, vp)
        mixed.append(jnp.concatenate(mixed_rows, axis=0))
    oa[:width, :] = jnp.concatenate(mixed, axis=1).astype(BF16)
    x1 = x + mm(wot[...], oa[...])
    xhat2, rstd2 = norm(x1)
    n2a[:width, :] = (xhat2 * gain2 + bias2).astype(BF16)
    z = mm(w1t[...], n2a[...])
    part_a, part_b = z[:FH], z[FH:]
    sigm = 1.0 / (1.0 + jnp.exp2(part_b * -log2e))
    silu = part_b * sigm
    ha[:FH, :] = (part_a * silu).astype(BF16)
    y = (x1 + mm(w2t[...], ha[:FH, :]) + bias_c2).astype(BF16)
    for g in range(group):
        y_ref[g] = y[:, g * LANES : g * LANES + length]

    gt = jnp.concatenate([wide(g_ref, g) for g in range(group)], axis=1)
    g2_ref[...] += mm(ha[...], gt, NT)
    dh = mm(w2_ref[...], gt)
    da = dh * silu
    db = dh * part_a * sigm * (1.0 + part_b * (1.0 - sigm))
    dz = jnp.concatenate([da, db], axis=0).astype(BF16)
    g1_ref[...] += mm(n2a[:208, :], dz, NT)
    dn2 = mm(w1_ref[...], dz)
    dx1 = gt.astype(F32) + norm_back(dn2, xhat2, rstd2, gain2, 1)
    da1 = dx1.astype(BF16)
    go_ref[...] += mm(oa[:208, :], da1, NT)
    do = mm(wo_ref[...], da1).astype(BF16).astype(F32)

    parts = []
    for g in range(group):
        sl = slice(g * LANES, (g + 1) * LANES)
        dqs, dks, dvs = [], [], []
        for p in range(H // 2):
            ds_ = []
            for j in range(2):
                h = 2 * p + j
                inv, o = kept[g * H + h][:2]
                d = do[h * head : (h + 1) * head, sl]
                low = jnp.sum(d * o, 0, keepdims=True) * -inv
                hi = low.astype(BF16).astype(F32)
                lo = low - hi
                tail = jnp.where(sub == 0, hi, jnp.where(sub == 1, lo, 0.0))
                ds_.append(padded(d * inv, tail))
            qd, kp, vp = kept[g * H + 2 * p + 1][2:]
            dd = pair_diag(*ds_)
            e = e_s[g, p]
            dpd = mm(vp.T, dd)
            dsc = (e.astype(F32) * dpd).astype(BF16)
            dv = mm(dd, e, NT)
            dq = mm(kp, dsc)
            dk = mm(qd, dsc, NT)
            for j in range(2):
                dqs.append(dq[32 * j : 32 * j + head, j * LANES : (j + 1) * LANES] * factor)
                dks.append(dk[32 * j : 32 * j + head] * factor)
                dvs.append(dv[32 * j : 32 * j + head])
        parts.append(jnp.concatenate(dqs + dks + dvs, axis=0))
    dqkv = jnp.concatenate(parts, axis=1).astype(BF16)
    gqkv_ref[...] += mm(n1a[:208, :], dqkv, NT)
    dn1 = mm(wqkv_ref[...], dqkv)
    dx = (dx1 + norm_back(dn1, xhat1, rstd1, gain1, 0)).astype(BF16)
    for g in range(group):
        dx_ref[g] = dx[:, g * LANES : g * LANES + length]

    @pl.when(step == pl.num_programs(0) - 1)
    def _():
        rows = [jnp.sum(ln_acc[i].T, 0, keepdims=True) for i in range(4)]
        vec = jnp.concatenate(
            [rows[0], rows[1], gqkv_ref[width : width + 1, :width], gqkv_ref[width : width + 1, 2 * width :],
             go_ref[width : width + 1], rows[2], rows[3], g2_ref[FH : FH + 1], g1_ref[width : width + 1]],
            axis=1,
        )
        shards, block_rows, _ = packed_ref.shape
        depth = width // shards
        extra = block_rows - depth
        per_vec = vec.shape[1] // shards
        pack_s[...] = jnp.zeros_like(pack_s)
        for w in range(shards):
            r = slice(w * depth, (w + 1) * depth)
            pack_s[w, :depth, : 4 * width] = jnp.concatenate([gqkv_ref[r, :], go_ref[r, :]], axis=1)
            pack_s[w, :depth, 4 * width :] = g1_ref[r, :]
            at = 4 * w * extra
            pack_s[w, depth:, : 4 * width] = jnp.concatenate(
                [g2_ref[at + j * extra : at + (j + 1) * extra, :] for j in range(4)], axis=1
            )
            pack_s[w, depth : depth + 1, 4 * width : 4 * width + per_vec] = vec[:, w * per_vec : (w + 1) * per_vec]
        packed_ref[...] = pack_s[...].astype(BF16)


def run_layer(x, mask, dout, full, group):
    samples, width, length = x.shape
    tokens = group * LANES
    whole = lambda a: pl.BlockSpec(a.shape, lambda i: (0,) * a.ndim)
    per = pl.BlockSpec((group, width, length), lambda i: (i, 0, 0))
    return pl.pallas_call(
        functools.partial(layer_kernel, group),
        grid=(samples // group,),
        in_specs=[per, whole(mask), per, whole(full)],
        out_specs=[per, per, whole(full)],
        out_shape=[jax.ShapeDtypeStruct(x.shape, BF16)] * 2 + [jax.ShapeDtypeStruct(full.shape, BF16)],
        scratch_shapes=[
            pltpu.VMEM((width, 4 * width + 2 * FH), F32),
            pltpu.VMEM((FH, width), F32),
            pltpu.VMEM((1, 8 * width + 2 * FH), F32),
            pltpu.VMEM((width, 3 * width), BF16),
            pltpu.VMEM((width, width), BF16),
            pltpu.VMEM((width, 2 * FH), BF16),
            pltpu.VMEM((FH, width), BF16),
            pltpu.VMEM((3 * width, 256), BF16),
            pltpu.VMEM((width, 256), BF16),
            pltpu.VMEM((2 * FH, 256), BF16),
            pltpu.VMEM((width, FH), BF16),
            pltpu.VMEM((5, width, LANES), F32),
            pltpu.VMEM((256, tokens), BF16),
            pltpu.VMEM((256, tokens), BF16),
            pltpu.VMEM((256, tokens), BF16),
            pltpu.VMEM((272, tokens), BF16),
            pltpu.VMEM((group, H // 2, LANES, 2 * LANES), BF16),
            pltpu.VMEM((208, 3 * width), F32),
            pltpu.VMEM((208, width), F32),
            pltpu.VMEM((208, 2 * FH), F32),
            pltpu.VMEM((272, width), F32),
            pltpu.VMEM((4, width, LANES), F32),
            pltpu.VMEM(full.shape, F32),
        ],
        compiler_params=pltpu.CompilerParams(vmem_limit_bytes=60 * 1024 * 1024),
        name="layer",
    )(x, mask, dout, full)


def send(src, dst, send_sem, recv_sem, device):
    copy = pltpu.make_async_remote_copy(
        src_ref=src, dst_ref=dst, send_sem=send_sem, recv_sem=recv_sem,
        device_id=device, device_id_type=pl.DeviceIdType.MESH,
    )
    copy.start()
    return copy


def meet(devices):
    barrier = pltpu.get_barrier_semaphore()
    for device in devices:
        pl.semaphore_signal(barrier, inc=1, device_id=device, device_id_type=pl.DeviceIdType.MESH)
    pl.semaphore_wait(barrier, len(devices))


def gather_kernel(n, attn_ref, w1_ref, w2_ref, vec_ref, out_ref, send1, recv1, send2, recv2):
    me = lax.axis_index("wide")
    core, chip, chips = lax.rem(me, 2), lax.div(me, 2), n // 2
    peer = lambda k: 2 * lax.rem(chip + k, chips) + core
    sibling = {"wide": me + 1 - 2 * core}
    depth = attn_ref.shape[0]
    width = attn_ref.shape[2]
    extra = w2_ref.shape[0] // 4
    lanes = out_ref.shape[2]
    top = jnp.concatenate([attn_ref[:, i, :] for i in range(4)] + [w1_ref[...]], axis=1)
    bottom = jnp.concatenate(
        [w2_ref[j * extra : (j + 1) * extra, :] for j in range(4)]
        + [jnp.broadcast_to(vec_ref[...], (extra, vec_ref.shape[1])),
           jnp.zeros((extra, lanes - 4 * width - vec_ref.shape[1]), F32)],
        axis=1,
    )
    out_ref[me] = jnp.concatenate([top, bottom], axis=0).astype(BF16)
    meet([{"wide": peer(k)} for k in range(1, chips)] + [sibling])
    mine = out_ref.at[me]
    copies = [send(mine, mine, send1.at[k], recv1.at[k], {"wide": peer(k)}) for k in range(1, chips)]
    passed = [send(mine, mine, send2.at[0], recv2.at[0], sibling)]
    for k in range(1, chips):
        copies[k - 1].wait_recv()
        block = out_ref.at[peer(chips - k)]
        passed.append(send(block, block, send2.at[k], recv2.at[k], sibling))
    for copy in copies:
        copy.wait_send()
    for copy in passed:
        copy.wait()


def gather(attn, w1, w2, vec, n):
    rows = attn.shape[0] + w2.shape[0] // 4
    lanes = 4 * attn.shape[2] + w1.shape[1]
    sems = pltpu.SemaphoreType.DMA((n // 2,))
    return pl.pallas_call(
        functools.partial(gather_kernel, n),
        out_shape=jax.ShapeDtypeStruct((n, rows, lanes), BF16),
        in_specs=[pl.BlockSpec(memory_space=pltpu.VMEM)] * 4,
        out_specs=pl.BlockSpec(memory_space=pltpu.VMEM),
        scratch_shapes=[sems] * 4,
        compiler_params=pltpu.CompilerParams(collective_id=0, has_side_effects=True),
        name="gather",
    )(attn, w1, w2, vec)


def reduce_kernel(n, copies_of, part_ref, out_ref, core_buf, sum_buf, wide_buf, narrow_buf,
                  send0, recv0, send1, recv1, send2, recv2):
    me, mine = lax.axis_index("wide"), lax.axis_index("narrow")
    core, chip, chips = lax.rem(me, 2), lax.div(me, 2), n // 2
    peer = lambda k: 2 * lax.rem(chip + k, chips) + core
    sibling = {"wide": me + 1 - 2 * core}
    twin = lambda j: {"narrow": lax.rem(mine + j, copies_of)}
    meet([{"wide": peer(k)} for k in range(1, chips)] + [sibling] + [twin(j) for j in range(1, copies_of)])
    order = list(range(1, chips)) + [0]
    first = {}
    for k in order:
        other = peer(k) + 1 - 2 * core
        first[k] = send(part_ref.at[other], core_buf.at[k], send0.at[k], recv0.at[k], sibling)
    second = {}
    for k in order:
        first[k].wait_recv()
        total = part_ref[peer(k)].astype(F32) + core_buf[k].astype(F32)
        if k:
            sum_buf[k] = total.astype(BF16)
            second[k] = send(sum_buf.at[k], wide_buf.at[k], send1.at[k], recv1.at[k], {"wide": peer(k)})
    for k in range(1, chips):
        second[k].wait_recv()
        total = total + wide_buf[k].astype(F32)
    narrow_buf[mine] = total
    third = [
        send(narrow_buf.at[mine], narrow_buf.at[mine], send2.at[j], recv2.at[j], twin(j))
        for j in range(1, copies_of)
    ]
    for copy in third:
        copy.wait_recv()
    result = narrow_buf[0]
    for j in range(1, copies_of):
        result = result + narrow_buf[j]
    out_ref[...] = result
    for copy in list(first.values()) + list(second.values()) + third:
        copy.wait_send()


def reduce_shares(packed, n, copies_of):
    chips = n // 2
    block = packed.shape[1:]
    sems = pltpu.SemaphoreType.DMA((chips,))
    few = pltpu.SemaphoreType.DMA((copies_of,))
    return pl.pallas_call(
        functools.partial(reduce_kernel, n, copies_of),
        out_shape=jax.ShapeDtypeStruct(block, F32),
        in_specs=[pl.BlockSpec(memory_space=pltpu.VMEM)],
        out_specs=pl.BlockSpec(memory_space=pltpu.VMEM),
        scratch_shapes=[pltpu.VMEM((chips,) + block, BF16)] * 3
        + [pltpu.VMEM((copies_of,) + block, F32), sems, sems, sems, sems, few, few],
        compiler_params=pltpu.CompilerParams(collective_id=1, has_side_effects=True),
        name="reduce",
    )(packed)


def adamw(weight, first_m, second_m, grad, decay):
    new_m = 0.9 * first_m + 0.1 * grad
    new_v = 0.999 * second_m + 0.001 * grad * grad
    ratio = new_m / (1.0 - 0.9**STEP) / (jnp.sqrt(new_v / (1.0 - 0.999**STEP)) + 1e-08)
    return (weight - 0.1 * (ratio + decay * weight), new_m, new_v)


def update_kernel(grad_ref, *refs):
    ins, outs = refs[:12], refs[12:]
    width = ins[0].shape[2]
    depth = ins[0].shape[0]
    extra = ins[6].shape[0] // 4

    def step(base, index, grad, decay):
        for ref, value in zip(outs[base : base + 3], adamw(*(r[index] for r in ins[base : base + 3]), grad, decay)):
            ref[index] = value

    for i in range(4):
        step(0, (slice(None), i, slice(None)), grad_ref[:depth, i * width : (i + 1) * width], 0.01)
    step(3, (slice(None), slice(None)), grad_ref[:depth, 4 * width :], 0.01)
    for j in range(4):
        step(6, (slice(j * extra, (j + 1) * extra), slice(None)), grad_ref[depth:, j * width : (j + 1) * width], 0.01)
    per_vec = ins[9].shape[1]
    step(9, (slice(None), slice(None)), grad_ref[depth : depth + 1, 4 * width : 4 * width + per_vec], 0.0)


def update(grad, states):
    vmem = pl.BlockSpec(memory_space=pltpu.VMEM)
    return pl.pallas_call(
        update_kernel,
        out_shape=[jax.ShapeDtypeStruct(a.shape, F32) for a in states],
        in_specs=[vmem] * 13,
        out_specs=[vmem] * 12,
        name="update",
    )(grad, *states)


def on_device(layer_input, mask, dout, attn_w, ffn_in, ffn_out, vec,
              m_attn, v_attn, m_in, v_in, m_out, v_out, m_vec, v_vec):
    n, copies_of = lax.axis_size("wide"), lax.axis_size("narrow")
    turn = lambda a: a.transpose(1, 0, 2)
    row = lambda a: a.reshape(1, -1)
    full = gather(turn(attn_w), ffn_in, ffn_out, row(vec), n)
    y, dx, packed = run_layer(layer_input.transpose(0, 2, 1), mask, dout.transpose(0, 2, 1), full, GROUP)
    share = reduce_shares(packed, n, copies_of)
    new = update(share, [turn(attn_w), turn(m_attn), turn(v_attn), ffn_in, m_in, v_in, ffn_out, m_out, v_out,
                         row(vec), row(m_vec), row(v_vec)])
    return (y.transpose(0, 2, 1), dx.transpose(0, 2, 1), *(turn(a) for a in new[:3]), *new[3:9],
            *(a.reshape(-1) for a in new[9:]))


def solution(mesh):
    rows = P(("wide", "narrow"), None, None)
    states = [P(None, "wide", None), P("wide", None), P("wide", None), P("wide")]
    moments = [s for s in states for _ in range(2)]
    results = [s for s in states for _ in range(3)]
    return jax.shard_map(
        on_device,
        mesh=mesh,
        in_specs=tuple([rows, P(("wide", "narrow"), None), rows] + states + moments),
        out_specs=tuple([rows, rows] + results),
        check_vma=False,
    )
```

```python
import functools
import jax
import jax.numpy as jnp
from jax import lax
from jax.experimental import pallas as pl
from jax.experimental.pallas import tpu as pltpu
from jax.sharding import PartitionSpec as P

H = 8
FH = 256
STEP = 10
LANES = 128
FORWARD = (0, 1, 7, 8, 9, 12)
BACKWARD = (0, 1, 5, 6, 9)
GROUP = 16
F32 = jnp.float32
BF16 = jnp.bfloat16
NN = (((1,), (0,)), ((), ()))
NT = (((1,), (1,)), ((), ()))


def mm(a, b, dims=NN):
    return lax.dot_general(a, b, dims, preferred_element_type=F32)


def layer_kernel(
    group,
    x_ref, mask_ref, g_ref, full_ref,
    y_ref, dx_ref, packed_ref,
    big, w2f, vec_s, wqkv_ref, wo_ref, w1_ref, w2_ref,
    wqkvt, wot, w1t, w2t, cols, n1a, n2a, oa, ha, e_s,
    gqkv_ref, go_ref, g1_ref, g2_ref, ln_acc, pack_s,
    q_s, k_s, v_s, d_s, c_s, dqkv_s, o_s, inv_s,
):
    step = pl.program_id(0)
    length = x_ref.shape[2]
    width = x_ref.shape[1]
    head = width // H
    tokens = group * LANES
    factor = float(head) ** (-0.5)
    log2e = 1.4426950408889634

    @pl.when(step == 0)
    def _():
        shards, block_rows, _ = full_ref.shape
        depth = width // shards
        extra = block_rows - depth
        per_vec = vec_s.shape[1] // shards
        for w in range(shards):
            block = full_ref[w].astype(F32)
            big[w * depth : (w + 1) * depth, :] = block[:depth]
            for j in range(4):
                at = (4 * w + j) * extra
                w2f[at : at + extra, :] = block[depth:, j * width : (j + 1) * width]
            vec_s[:, w * per_vec : (w + 1) * per_vec] = block[depth : depth + 1, 4 * width : 4 * width + per_vec]
        wqkv_ref[...] = big[:, : 3 * width].astype(BF16)
        wo_ref[...] = big[:, 3 * width : 4 * width].astype(BF16)
        w1_ref[...] = big[:, 4 * width :].astype(BF16)
        w2_ref[...] = w2f[...].astype(BF16)

        def aug(w, bias):
            rows = lax.broadcasted_iota(jnp.int32, (64, w.shape[1]), 0)
            tail = jnp.where(rows == 0, jnp.broadcast_to(bias, (64, w.shape[1])), 0.0)
            return jnp.concatenate([w.astype(F32), tail], axis=0).T.astype(BF16)

        zero_row = jnp.zeros((1, width), F32)
        v = vec_s[...]
        piece = lambda i: v[:, i * width : (i + 1) * width]
        bias_qkv = jnp.concatenate([piece(2), zero_row, piece(3)], axis=1)
        wqkvt[...] = aug(wqkv_ref[...], bias_qkv)
        wot[...] = aug(wo_ref[...], piece(4))
        w1t[...] = aug(w1_ref[...], v[:, 8 * width : 8 * width + 2 * FH])
        w2t[...] = w2_ref[...].astype(F32).T.astype(BF16)
        for j, i in enumerate((0, 1, 5, 6, 7)):
            cols[j] = jnp.broadcast_to(piece(i), (LANES, width)).T
        rows = lax.broadcasted_iota(jnp.int32, (64, tokens), 0)
        one = jnp.where(rows == 0, 1.0, 0.0).astype(BF16)
        n1a[width:, :] = one
        n2a[width:, :] = one
        oa[width:, :] = one
        ha[FH:, :] = one[:16]
        gqkv_ref[...] = jnp.zeros_like(gqkv_ref)
        go_ref[...] = jnp.zeros_like(go_ref)
        g1_ref[...] = jnp.zeros_like(g1_ref)
        g2_ref[...] = jnp.zeros_like(g2_ref)
        ln_acc[...] = jnp.zeros_like(ln_acc)

    def wide(ref, g):
        t = ref[g]
        return jnp.concatenate([t, jnp.zeros((width, LANES - length), t.dtype)], axis=1)

    def tile(col):
        return jnp.concatenate([col] * group, axis=1) if group > 1 else col

    def norm(value):
        center = value - jnp.sum(value, 0, keepdims=True) * (1.0 / width)
        rstd = lax.rsqrt(jnp.sum(center * center, 0, keepdims=True) * (1.0 / width) + 1e-05)
        return center * rstd, rstd

    def norm_back(dn, xhat, rstd, gain, which):
        prod = dn * xhat
        a0, a1 = ln_acc[2 * which], ln_acc[2 * which + 1]
        for g in range(group):
            sl = slice(g * LANES, (g + 1) * LANES)
            a0 = a0 + prod[:, sl]
            a1 = a1 + dn[:, sl]
        ln_acc[2 * which] = a0
        ln_acc[2 * which + 1] = a1
        t = dn * gain
        m1 = jnp.sum(t, 0, keepdims=True) * (1.0 / width)
        m2 = jnp.sum(t * xhat, 0, keepdims=True) * (1.0 / width)
        return rstd * (t - m1 - xhat * m2)

    gain1, bias1, gain2, bias2, bias_c2 = (tile(cols[j]) for j in range(5))

    x = jnp.concatenate([wide(x_ref, g) for g in range(group)], axis=1).astype(F32)
    xhat1, rstd1 = norm(x)
    n1a[:width, :] = (xhat1 * gain1 + bias1).astype(BF16)
    qkv = mm(wqkvt[...], n1a[...])

    sub = lax.broadcasted_iota(jnp.int32, (16, LANES), 0)
    lane = lax.broadcasted_iota(jnp.int32, (16, LANES), 1)
    ones_q = jnp.where(sub == 0, 1.0, 0.0)
    ones_v = jnp.where(sub < 2, 1.0, 0.0)
    empty = jnp.zeros((head, LANES), F32)
    two = 2 * head
    live = {}

    def block_diag(first, second, tail_first, tail_second):
        left = jnp.concatenate([first, empty, tail_first], axis=0).astype(BF16)
        right = jnp.concatenate([empty, second, tail_second], axis=0).astype(BF16)
        return jnp.concatenate([left, right], axis=1)

    def run(stages, lags):
        items = [(g, p) for g in range(group) for p in range(H // 2)]
        for t in range(len(items) + max(lags)):
            for stage, lag in reversed(list(zip(stages, lags))):
                if 0 <= t - lag < len(items):
                    stage(t - lag, *items[t - lag])

    def forward_prepare(t, g, p):
        sl = slice(g * LANES, (g + 1) * LANES)
        m = mask_ref[pl.ds(step * group + g, 1), :]
        m = jnp.concatenate([m, jnp.zeros((1, LANES - length), jnp.int32)], axis=1)
        ok = (jnp.broadcast_to(m, (16, LANES)) != 0) | (lane == 0)
        tail_k = jnp.where((sub == 0) & jnp.logical_not(ok), -1e30, 0.0)
        lo = p * two
        q_s[g, p] = block_diag(qkv[lo : lo + head, sl], qkv[lo + head : lo + two, sl], ones_q, ones_q)
        kp = jnp.concatenate([qkv[width + lo : width + lo + two, sl], tail_k], axis=0).astype(BF16)
        k_s[g, p] = kp
        v_s[g, p] = jnp.concatenate([qkv[2 * width + lo : 2 * width + lo + two, sl], ones_v], axis=0).astype(BF16)
        live["k", t] = kp.T

    def forward_scores(t, g, p):
        live["s", t] = mm(live.pop(("k", t)), q_s[g, p])

    def forward_top(t, g, p):
        live["m", t] = jnp.max(live["s", t], 0, keepdims=True)

    def forward_exp(t, g, p):
        e_s[g, p] = jnp.exp2((live.pop(("s", t)) - live.pop(("m", t))) * (factor * log2e)).astype(BF16)

    def forward_mix(t, g, p):
        live["n", t] = mm(v_s[g, p], e_s[g, p])

    def forward_out(t, g, p):
        num = live.pop(("n", t))
        inv = 1.0 / num[two : two + 1]
        inv_s[g, p : p + 1, :] = inv
        sl = slice(g * LANES, (g + 1) * LANES)
        lo = p * two
        o_s[lo : lo + head, sl] = num[:head, :LANES] * inv[:, :LANES]
        o_s[lo + head : lo + two, sl] = num[head:two, LANES:] * inv[:, LANES:]

    run([forward_prepare, forward_scores, forward_top, forward_exp, forward_mix, forward_out], FORWARD)
    oa[:width, :] = o_s[...].astype(BF16)
    x1 = x + mm(wot[...], oa[...])
    xhat2, rstd2 = norm(x1)
    n2a[:width, :] = (xhat2 * gain2 + bias2).astype(BF16)
    z = mm(w1t[...], n2a[...])
    part_a, part_b = z[:FH], z[FH:]
    sigm = 1.0 / (1.0 + jnp.exp2(part_b * -log2e))
    silu = part_b * sigm
    ha[:FH, :] = (part_a * silu).astype(BF16)
    y = (x1 + mm(w2t[...], ha[:FH, :]) + bias_c2).astype(BF16)
    for g in range(group):
        y_ref[g] = y[:, g * LANES : g * LANES + length]

    gt = jnp.concatenate([wide(g_ref, g) for g in range(group)], axis=1)
    g2_ref[...] += mm(ha[...], gt, NT)
    dh = mm(w2_ref[...], gt)
    da = dh * silu
    db = dh * part_a * sigm * (1.0 + part_b * (1.0 - sigm))
    dz = jnp.concatenate([da, db], axis=0).astype(BF16)
    g1_ref[...] += mm(n2a[:208, :], dz, NT)
    dn2 = mm(w1_ref[...], dz)
    dx1 = gt.astype(F32) + norm_back(dn2, xhat2, rstd2, gain2, 1)
    da1 = dx1.astype(BF16)
    go_ref[...] += mm(oa[:208, :], da1, NT)
    do = mm(wo_ref[...], da1).astype(BF16).astype(F32)

    def backward_prepare(t, g, p):
        sl = slice(g * LANES, (g + 1) * LANES)
        rows, tails = [], []
        for j in range(2):
            r = slice(p * two + j * head, p * two + (j + 1) * head)
            d = do[r, sl]
            inv = inv_s[g, p : p + 1, j * LANES : (j + 1) * LANES]
            low = jnp.sum(d * o_s[r, sl], 0, keepdims=True) * -inv
            hi = low.astype(BF16).astype(F32)
            rows.append(d * inv)
            tails.append(jnp.where(sub == 0, hi, jnp.where(sub == 1, low - hi, 0.0)))
        d_s[g, p] = block_diag(*rows, *tails)
        live["v", t] = v_s[g, p].T

    def backward_probs(t, g, p):
        live["p", t] = mm(live.pop(("v", t)), d_s[g, p])

    def backward_scores(t, g, p):
        c_s[g, p] = (e_s[g, p].astype(F32) * live.pop(("p", t))).astype(BF16)

    def backward_mix(t, g, p):
        live["dv", t] = mm(d_s[g, p, :two], e_s[g, p], NT)
        live["dk", t] = mm(q_s[g, p, :two], c_s[g, p], NT)
        live["dq", t] = mm(k_s[g, p, :two], c_s[g, p])

    def backward_out(t, g, p):
        sl = slice(g * LANES, (g + 1) * LANES)
        lo = p * two
        dq = live.pop(("dq", t))
        dq = jnp.concatenate([dq[:head, :LANES], dq[head:, LANES:]], axis=0)
        dqkv_s[lo : lo + two, sl] = (dq * factor).astype(BF16)
        dqkv_s[width + lo : width + lo + two, sl] = (live.pop(("dk", t)) * factor).astype(BF16)
        dqkv_s[2 * width + lo : 2 * width + lo + two, sl] = live.pop(("dv", t)).astype(BF16)

    run([backward_prepare, backward_probs, backward_scores, backward_mix, backward_out], BACKWARD)
    dqkv = dqkv_s[...]
    gqkv_ref[...] += mm(n1a[:208, :], dqkv, NT)
    dn1 = mm(wqkv_ref[...], dqkv)
    dx = (dx1 + norm_back(dn1, xhat1, rstd1, gain1, 0)).astype(BF16)
    for g in range(group):
        dx_ref[g] = dx[:, g * LANES : g * LANES + length]

    @pl.when(step == pl.num_programs(0) - 1)
    def _():
        rows = [jnp.sum(ln_acc[i].T, 0, keepdims=True) for i in range(4)]
        vec = jnp.concatenate(
            [rows[0], rows[1], gqkv_ref[width : width + 1, :width], gqkv_ref[width : width + 1, 2 * width :],
             go_ref[width : width + 1], rows[2], rows[3], g2_ref[FH : FH + 1], g1_ref[width : width + 1]],
            axis=1,
        )
        shards, block_rows, _ = packed_ref.shape
        depth = width // shards
        extra = block_rows - depth
        per_vec = vec.shape[1] // shards
        pack_s[...] = jnp.zeros_like(pack_s)
        for w in range(shards):
            r = slice(w * depth, (w + 1) * depth)
            pack_s[w, :depth, : 4 * width] = jnp.concatenate([gqkv_ref[r, :], go_ref[r, :]], axis=1)
            pack_s[w, :depth, 4 * width :] = g1_ref[r, :]
            at = 4 * w * extra
            pack_s[w, depth:, : 4 * width] = jnp.concatenate(
                [g2_ref[at + j * extra : at + (j + 1) * extra, :] for j in range(4)], axis=1
            )
            pack_s[w, depth : depth + 1, 4 * width : 4 * width + per_vec] = vec[:, w * per_vec : (w + 1) * per_vec]
        packed_ref[...] = pack_s[...].astype(BF16)


def run_layer(x, mask, dout, full, group):
    samples, width, length = x.shape
    tokens = group * LANES
    whole = lambda a: pl.BlockSpec(a.shape, lambda i: (0,) * a.ndim)
    per = pl.BlockSpec((group, width, length), lambda i: (i, 0, 0))
    return pl.pallas_call(
        functools.partial(layer_kernel, group),
        grid=(samples // group,),
        in_specs=[per, whole(mask), per, whole(full)],
        out_specs=[per, per, whole(full)],
        out_shape=[jax.ShapeDtypeStruct(x.shape, BF16)] * 2 + [jax.ShapeDtypeStruct(full.shape, BF16)],
        scratch_shapes=[
            pltpu.VMEM((width, 4 * width + 2 * FH), F32),
            pltpu.VMEM((FH, width), F32),
            pltpu.VMEM((1, 8 * width + 2 * FH), F32),
            pltpu.VMEM((width, 3 * width), BF16),
            pltpu.VMEM((width, width), BF16),
            pltpu.VMEM((width, 2 * FH), BF16),
            pltpu.VMEM((FH, width), BF16),
            pltpu.VMEM((3 * width, 256), BF16),
            pltpu.VMEM((width, 256), BF16),
            pltpu.VMEM((2 * FH, 256), BF16),
            pltpu.VMEM((width, FH), BF16),
            pltpu.VMEM((5, width, LANES), F32),
            pltpu.VMEM((256, tokens), BF16),
            pltpu.VMEM((256, tokens), BF16),
            pltpu.VMEM((256, tokens), BF16),
            pltpu.VMEM((272, tokens), BF16),
            pltpu.VMEM((group, H // 2, LANES, 2 * LANES), BF16),
            pltpu.VMEM((208, 3 * width), F32),
            pltpu.VMEM((208, width), F32),
            pltpu.VMEM((208, 2 * FH), F32),
            pltpu.VMEM((272, width), F32),
            pltpu.VMEM((4, width, LANES), F32),
            pltpu.VMEM(full.shape, F32),
            pltpu.VMEM((group, H // 2, 64, 2 * LANES), BF16),
            pltpu.VMEM((group, H // 2, 64, LANES), BF16),
            pltpu.VMEM((group, H // 2, 64, LANES), BF16),
            pltpu.VMEM((group, H // 2, 64, 2 * LANES), BF16),
            pltpu.VMEM((group, H // 2, LANES, 2 * LANES), BF16),
            pltpu.VMEM((3 * width, tokens), BF16),
            pltpu.VMEM((width, tokens), F32),
            pltpu.VMEM((group, H // 2, 2 * LANES), F32),
        ],
        compiler_params=pltpu.CompilerParams(vmem_limit_bytes=60 * 1024 * 1024),
        name="layer",
    )(x, mask, dout, full)


def send(src, dst, send_sem, recv_sem, device):
    copy = pltpu.make_async_remote_copy(
        src_ref=src, dst_ref=dst, send_sem=send_sem, recv_sem=recv_sem,
        device_id=device, device_id_type=pl.DeviceIdType.MESH,
    )
    copy.start()
    return copy


def meet(devices):
    barrier = pltpu.get_barrier_semaphore()
    for device in devices:
        pl.semaphore_signal(barrier, inc=1, device_id=device, device_id_type=pl.DeviceIdType.MESH)
    pl.semaphore_wait(barrier, len(devices))


def gather_kernel(n, attn_ref, w1_ref, w2_ref, vec_ref, out_ref, send1, recv1, send2, recv2):
    me = lax.axis_index("wide")
    core, chip, chips = lax.rem(me, 2), lax.div(me, 2), n // 2
    peer = lambda k: 2 * lax.rem(chip + k, chips) + core
    sibling = {"wide": me + 1 - 2 * core}
    depth = attn_ref.shape[0]
    width = attn_ref.shape[2]
    extra = w2_ref.shape[0] // 4
    lanes = out_ref.shape[2]
    top = jnp.concatenate([attn_ref[:, i, :] for i in range(4)] + [w1_ref[...]], axis=1)
    bottom = jnp.concatenate(
        [w2_ref[j * extra : (j + 1) * extra, :] for j in range(4)]
        + [jnp.broadcast_to(vec_ref[...], (extra, vec_ref.shape[1])),
           jnp.zeros((extra, lanes - 4 * width - vec_ref.shape[1]), F32)],
        axis=1,
    )
    out_ref[me] = jnp.concatenate([top, bottom], axis=0).astype(BF16)
    meet([{"wide": peer(k)} for k in range(1, chips)] + [sibling])
    mine = out_ref.at[me]
    copies = [send(mine, mine, send1.at[k], recv1.at[k], {"wide": peer(k)}) for k in range(1, chips)]
    passed = [send(mine, mine, send2.at[0], recv2.at[0], sibling)]
    for k in range(1, chips):
        copies[k - 1].wait_recv()
        block = out_ref.at[peer(chips - k)]
        passed.append(send(block, block, send2.at[k], recv2.at[k], sibling))
    for copy in copies:
        copy.wait_send()
    for copy in passed:
        copy.wait()


def gather(attn, w1, w2, vec, n):
    rows = attn.shape[0] + w2.shape[0] // 4
    lanes = 4 * attn.shape[2] + w1.shape[1]
    sems = pltpu.SemaphoreType.DMA((n // 2,))
    return pl.pallas_call(
        functools.partial(gather_kernel, n),
        out_shape=jax.ShapeDtypeStruct((n, rows, lanes), BF16),
        in_specs=[pl.BlockSpec(memory_space=pltpu.VMEM)] * 4,
        out_specs=pl.BlockSpec(memory_space=pltpu.VMEM),
        scratch_shapes=[sems] * 4,
        compiler_params=pltpu.CompilerParams(collective_id=0, has_side_effects=True),
        name="gather",
    )(attn, w1, w2, vec)


def reduce_kernel(n, copies_of, part_ref, out_ref, core_buf, sum_buf, wide_buf, narrow_buf,
                  send0, recv0, send1, recv1, send2, recv2):
    me, mine = lax.axis_index("wide"), lax.axis_index("narrow")
    core, chip, chips = lax.rem(me, 2), lax.div(me, 2), n // 2
    peer = lambda k: 2 * lax.rem(chip + k, chips) + core
    sibling = {"wide": me + 1 - 2 * core}
    twin = lambda j: {"narrow": lax.rem(mine + j, copies_of)}
    meet([{"wide": peer(k)} for k in range(1, chips)] + [sibling] + [twin(j) for j in range(1, copies_of)])
    order = list(range(1, chips)) + [0]
    first = {}
    for k in order:
        other = peer(k) + 1 - 2 * core
        first[k] = send(part_ref.at[other], core_buf.at[k], send0.at[k], recv0.at[k], sibling)
    second = {}
    for k in order:
        first[k].wait_recv()
        total = part_ref[peer(k)].astype(F32) + core_buf[k].astype(F32)
        if k:
            sum_buf[k] = total.astype(BF16)
            second[k] = send(sum_buf.at[k], wide_buf.at[k], send1.at[k], recv1.at[k], {"wide": peer(k)})
    for k in range(1, chips):
        second[k].wait_recv()
        total = total + wide_buf[k].astype(F32)
    narrow_buf[mine] = total
    third = [
        send(narrow_buf.at[mine], narrow_buf.at[mine], send2.at[j], recv2.at[j], twin(j))
        for j in range(1, copies_of)
    ]
    for copy in third:
        copy.wait_recv()
    result = narrow_buf[0]
    for j in range(1, copies_of):
        result = result + narrow_buf[j]
    out_ref[...] = result
    for copy in list(first.values()) + list(second.values()) + third:
        copy.wait_send()


def reduce_shares(packed, n, copies_of):
    chips = n // 2
    block = packed.shape[1:]
    sems = pltpu.SemaphoreType.DMA((chips,))
    few = pltpu.SemaphoreType.DMA((copies_of,))
    return pl.pallas_call(
        functools.partial(reduce_kernel, n, copies_of),
        out_shape=jax.ShapeDtypeStruct(block, F32),
        in_specs=[pl.BlockSpec(memory_space=pltpu.VMEM)],
        out_specs=pl.BlockSpec(memory_space=pltpu.VMEM),
        scratch_shapes=[pltpu.VMEM((chips,) + block, BF16)] * 3
        + [pltpu.VMEM((copies_of,) + block, F32), sems, sems, sems, sems, few, few],
        compiler_params=pltpu.CompilerParams(collective_id=1, has_side_effects=True),
        name="reduce",
    )(packed)


def adamw(weight, first_m, second_m, grad, decay):
    new_m = 0.9 * first_m + 0.1 * grad
    new_v = 0.999 * second_m + 0.001 * grad * grad
    ratio = new_m / (1.0 - 0.9**STEP) / (jnp.sqrt(new_v / (1.0 - 0.999**STEP)) + 1e-08)
    return (weight - 0.1 * (ratio + decay * weight), new_m, new_v)


def update_kernel(grad_ref, *refs):
    ins, outs = refs[:12], refs[12:]
    width = ins[0].shape[2]
    depth = ins[0].shape[0]
    extra = ins[6].shape[0] // 4

    def step(base, index, grad, decay):
        for ref, value in zip(outs[base : base + 3], adamw(*(r[index] for r in ins[base : base + 3]), grad, decay)):
            ref[index] = value

    for i in range(4):
        step(0, (slice(None), i, slice(None)), grad_ref[:depth, i * width : (i + 1) * width], 0.01)
    step(3, (slice(None), slice(None)), grad_ref[:depth, 4 * width :], 0.01)
    for j in range(4):
        step(6, (slice(j * extra, (j + 1) * extra), slice(None)), grad_ref[depth:, j * width : (j + 1) * width], 0.01)
    per_vec = ins[9].shape[1]
    step(9, (slice(None), slice(None)), grad_ref[depth : depth + 1, 4 * width : 4 * width + per_vec], 0.0)


def update(grad, states):
    vmem = pl.BlockSpec(memory_space=pltpu.VMEM)
    return pl.pallas_call(
        update_kernel,
        out_shape=[jax.ShapeDtypeStruct(a.shape, F32) for a in states],
        in_specs=[vmem] * 13,
        out_specs=[vmem] * 12,
        name="update",
    )(grad, *states)


def on_device(layer_input, mask, dout, attn_w, ffn_in, ffn_out, vec,
              m_attn, v_attn, m_in, v_in, m_out, v_out, m_vec, v_vec):
    n, copies_of = lax.axis_size("wide"), lax.axis_size("narrow")
    turn = lambda a: a.transpose(1, 0, 2)
    row = lambda a: a.reshape(1, -1)
    full = gather(turn(attn_w), ffn_in, ffn_out, row(vec), n)
    y, dx, packed = run_layer(layer_input.transpose(0, 2, 1), mask, dout.transpose(0, 2, 1), full, GROUP)
    share = reduce_shares(packed, n, copies_of)
    new = update(share, [turn(attn_w), turn(m_attn), turn(v_attn), ffn_in, m_in, v_in, ffn_out, m_out, v_out,
                         row(vec), row(m_vec), row(v_vec)])
    return (y.transpose(0, 2, 1), dx.transpose(0, 2, 1), *(turn(a) for a in new[:3]), *new[3:9],
            *(a.reshape(-1) for a in new[9:]))


def solution(mesh):
    rows = P(("wide", "narrow"), None, None)
    states = [P(None, "wide", None), P("wide", None), P("wide", None), P("wide")]
    moments = [s for s in states for _ in range(2)]
    results = [s for s in states for _ in range(3)]
    return jax.shard_map(
        on_device,
        mesh=mesh,
        in_specs=tuple([rows, P(("wide", "narrow"), None), rows] + states + moments),
        out_specs=tuple([rows, rows] + results),
        check_vma=False,
    )
```

```python
import functools
import jax
import jax.numpy as jnp
from jax import lax
from jax.experimental import pallas as pl
from jax.experimental.pallas import tpu as pltpu
from jax.sharding import PartitionSpec as P

H = 8
FH = 256
STEP = 10
LANES = 128
FORWARD = (0, 1, 7, 8, 9, 12)
BACKWARD = (0, 1, 1, 5, 6, 9)
GROUP = 16
F32 = jnp.float32
BF16 = jnp.bfloat16
NN = (((1,), (0,)), ((), ()))
NT = (((1,), (1,)), ((), ()))


def mm(a, b, dims=NN):
    return lax.dot_general(a, b, dims, preferred_element_type=F32)


def layer_kernel(
    group,
    x_ref, mask_ref, g_ref, full_ref,
    y_ref, dx_ref, packed_ref,
    big, w2f, vec_s, wqkv_ref, wo_ref, w1_ref, w2_ref,
    wqkvt, wot, w1t, w2t, cols, n1a, n2a, oa, ha, e_s,
    gqkv_ref, go_ref, g1_ref, g2_ref, ln_acc, pack_s, gqkvt_ref,
    q_s, k_s, v_s, d_s, c_s, dqkv_s, o_s, inv_s, et_s,
):
    step = pl.program_id(0)
    length = x_ref.shape[2]
    width = x_ref.shape[1]
    head = width // H
    tokens = group * LANES
    factor = float(head) ** (-0.5)
    log2e = 1.4426950408889634

    @pl.when(step == 0)
    def _():
        shards, _, block_rows, _ = full_ref.shape
        depth = width // shards
        extra = block_rows - depth
        per_vec = vec_s.shape[1] // shards
        for w in range(shards):
            block = jnp.concatenate([full_ref[w, 0], full_ref[w, 1]], axis=1).astype(F32)
            big[w * depth : (w + 1) * depth, :] = block[:depth]
            for j in range(4):
                at = (4 * w + j) * extra
                w2f[at : at + extra, :] = block[depth:, j * width : (j + 1) * width]
            vec_s[:, w * per_vec : (w + 1) * per_vec] = block[depth : depth + 1, 4 * width : 4 * width + per_vec]
        wqkv_ref[...] = big[:, : 3 * width].astype(BF16)
        wo_ref[...] = big[:, 3 * width : 4 * width].astype(BF16)
        w1_ref[...] = big[:, 4 * width :].astype(BF16)
        w2_ref[...] = w2f[...].astype(BF16)

        def aug(w, bias):
            rows = lax.broadcasted_iota(jnp.int32, (64, w.shape[1]), 0)
            tail = jnp.where(rows == 0, jnp.broadcast_to(bias, (64, w.shape[1])), 0.0)
            return jnp.concatenate([w.astype(F32), tail], axis=0).T.astype(BF16)

        zero_row = jnp.zeros((1, width), F32)
        v = vec_s[...]
        piece = lambda i: v[:, i * width : (i + 1) * width]
        bias_qkv = jnp.concatenate([piece(2), zero_row, piece(3)], axis=1)
        wqkvt[...] = aug(wqkv_ref[...], bias_qkv)
        wot[...] = aug(wo_ref[...], piece(4))
        w1t[...] = aug(w1_ref[...], v[:, 8 * width : 8 * width + 2 * FH])
        w2t[...] = w2_ref[...].astype(F32).T.astype(BF16)
        for j, i in enumerate((0, 1, 5, 6, 7)):
            cols[j] = jnp.broadcast_to(piece(i), (LANES, width)).T
        rows = lax.broadcasted_iota(jnp.int32, (64, tokens), 0)
        one = jnp.where(rows == 0, 1.0, 0.0).astype(BF16)
        n1a[width:, :] = one
        n2a[width:, :] = one
        oa[width:, :] = one
        ha[FH:, :] = one[:16]
        gqkvt_ref[...] = jnp.zeros_like(gqkvt_ref)
        go_ref[...] = jnp.zeros_like(go_ref)
        g1_ref[...] = jnp.zeros_like(g1_ref)
        g2_ref[...] = jnp.zeros_like(g2_ref)
        ln_acc[...] = jnp.zeros_like(ln_acc)

    def wide(ref, g):
        t = ref[g]
        return jnp.concatenate([t, jnp.zeros((width, LANES - length), t.dtype)], axis=1)

    def tile(col):
        return jnp.concatenate([col] * group, axis=1) if group > 1 else col

    def norm(value):
        center = value - jnp.sum(value, 0, keepdims=True) * (1.0 / width)
        rstd = lax.rsqrt(jnp.sum(center * center, 0, keepdims=True) * (1.0 / width) + 1e-05)
        return center * rstd, rstd

    def norm_back(dn, xhat, rstd, gain, which):
        prod = dn * xhat
        a0, a1 = ln_acc[2 * which], ln_acc[2 * which + 1]
        for g in range(group):
            sl = slice(g * LANES, (g + 1) * LANES)
            a0 = a0 + prod[:, sl]
            a1 = a1 + dn[:, sl]
        ln_acc[2 * which] = a0
        ln_acc[2 * which + 1] = a1
        t = dn * gain
        m1 = jnp.sum(t, 0, keepdims=True) * (1.0 / width)
        m2 = jnp.sum(t * xhat, 0, keepdims=True) * (1.0 / width)
        return rstd * (t - m1 - xhat * m2)

    gain1, bias1, gain2, bias2, bias_c2 = (tile(cols[j]) for j in range(5))

    x = jnp.concatenate([wide(x_ref, g) for g in range(group)], axis=1).astype(F32)
    xhat1, rstd1 = norm(x)
    n1a[:width, :] = (xhat1 * gain1 + bias1).astype(BF16)
    qkv = mm(wqkvt[...], n1a[...])

    sub = lax.broadcasted_iota(jnp.int32, (16, LANES), 0)
    lane = lax.broadcasted_iota(jnp.int32, (16, LANES), 1)
    ones_q = jnp.where(sub == 0, 1.0, 0.0)
    ones_v = jnp.where(sub < 2, 1.0, 0.0)
    empty = jnp.zeros((head, LANES), F32)
    two = 2 * head
    live = {}

    def block_diag(first, second, tail_first, tail_second):
        left = jnp.concatenate([first, empty, tail_first], axis=0).astype(BF16)
        right = jnp.concatenate([empty, second, tail_second], axis=0).astype(BF16)
        return jnp.concatenate([left, right], axis=1)

    def run(stages, lags):
        items = [(g, p) for g in range(group) for p in range(H // 2)]
        for t in range(len(items) + max(lags)):
            for stage, lag in reversed(list(zip(stages, lags))):
                if 0 <= t - lag < len(items):
                    stage(t - lag, *items[t - lag])

    def forward_prepare(t, g, p):
        sl = slice(g * LANES, (g + 1) * LANES)
        m = mask_ref[pl.ds(step * group + g, 1), :]
        m = jnp.concatenate([m, jnp.zeros((1, LANES - length), jnp.int32)], axis=1)
        ok = (jnp.broadcast_to(m, (16, LANES)) != 0) | (lane == 0)
        tail_k = jnp.where((sub == 0) & jnp.logical_not(ok), -1e30, 0.0)
        lo = p * two
        q_s[g, p] = block_diag(qkv[lo : lo + head, sl], qkv[lo + head : lo + two, sl], ones_q, ones_q)
        kp = jnp.concatenate([qkv[width + lo : width + lo + two, sl], tail_k], axis=0).astype(BF16)
        k_s[g, p] = kp
        v_s[g, p] = jnp.concatenate([qkv[2 * width + lo : 2 * width + lo + two, sl], ones_v], axis=0).astype(BF16)
        live["k", t] = kp.T

    def forward_scores(t, g, p):
        live["s", t] = mm(live.pop(("k", t)), q_s[g, p])

    def forward_top(t, g, p):
        live["m", t] = jnp.max(live["s", t], 0, keepdims=True)

    def forward_exp(t, g, p):
        e_s[g, p] = jnp.exp2((live.pop(("s", t)) - live.pop(("m", t))) * (factor * log2e)).astype(BF16)

    def forward_mix(t, g, p):
        live["n", t] = mm(v_s[g, p], e_s[g, p])

    def forward_out(t, g, p):
        num = live.pop(("n", t))
        inv = 1.0 / num[two : two + 1]
        inv_s[g, p : p + 1, :] = inv
        sl = slice(g * LANES, (g + 1) * LANES)
        lo = p * two
        o_s[lo : lo + head, sl] = num[:head, :LANES] * inv[:, :LANES]
        o_s[lo + head : lo + two, sl] = num[head:two, LANES:] * inv[:, LANES:]

    run([forward_prepare, forward_scores, forward_top, forward_exp, forward_mix, forward_out], FORWARD)
    oa[:width, :] = o_s[...].astype(BF16)
    x1 = x + mm(wot[...], oa[...])
    xhat2, rstd2 = norm(x1)
    n2a[:width, :] = (xhat2 * gain2 + bias2).astype(BF16)
    z = mm(w1t[...], n2a[...])
    part_a, part_b = z[:FH], z[FH:]
    sigm = 1.0 / (1.0 + jnp.exp2(part_b * -log2e))
    silu = part_b * sigm
    ha[:FH, :] = (part_a * silu).astype(BF16)
    y = (x1 + mm(w2t[...], ha[:FH, :]) + bias_c2).astype(BF16)
    for g in range(group):
        y_ref[g] = y[:, g * LANES : g * LANES + length]

    gt = jnp.concatenate([wide(g_ref, g) for g in range(group)], axis=1)
    g2_ref[...] += mm(ha[...], gt, NT)
    dh = mm(w2_ref[...], gt)
    da = dh * silu
    db = dh * part_a * sigm * (1.0 + part_b * (1.0 - sigm))
    dz = jnp.concatenate([da, db], axis=0).astype(BF16)
    g1_ref[...] += mm(n2a[:208, :], dz, NT)
    dn2 = mm(w1_ref[...], dz)
    dx1 = gt.astype(F32) + norm_back(dn2, xhat2, rstd2, gain2, 1)
    da1 = dx1.astype(BF16)
    go_ref[...] += mm(oa[:208, :], da1, NT)
    do = mm(wo_ref[...], da1).astype(BF16).astype(F32)

    def backward_prepare(t, g, p):
        sl = slice(g * LANES, (g + 1) * LANES)
        rows, tails = [], []
        for j in range(2):
            r = slice(p * two + j * head, p * two + (j + 1) * head)
            d = do[r, sl]
            inv = inv_s[g, p : p + 1, j * LANES : (j + 1) * LANES]
            low = jnp.sum(d * o_s[r, sl], 0, keepdims=True) * -inv
            hi = low.astype(BF16).astype(F32)
            rows.append(d * inv)
            tails.append(jnp.where(sub == 0, hi, jnp.where(sub == 1, low - hi, 0.0)))
        d_s[g, p] = block_diag(*rows, *tails)
        live["v", t] = v_s[g, p].T
        live["r", t] = jnp.concatenate(rows, axis=0).astype(BF16)

    def backward_probs(t, g, p):
        live["p", t] = mm(live.pop(("v", t)), d_s[g, p])

    def backward_scores(t, g, p):
        c_s[g, p] = (e_s[g, p].astype(F32) * live.pop(("p", t))).astype(BF16)

    def backward_turn(t, g, p):
        e = e_s[g, p]
        et_s[g, p] = jnp.concatenate([e[:, :LANES].T, e[:, LANES:].T], axis=1)

    def backward_mix(t, g, p):
        live["dv", t] = mm(live.pop(("r", t)), et_s[g, p])
        live["dk", t] = mm(q_s[g, p, :two], c_s[g, p], NT)
        live["dq", t] = mm(k_s[g, p, :two], c_s[g, p])

    def backward_out(t, g, p):
        sl = slice(g * LANES, (g + 1) * LANES)
        lo = p * two
        dq = live.pop(("dq", t))
        dq = jnp.concatenate([dq[:head, :LANES], dq[head:, LANES:]], axis=0)
        dqkv_s[lo : lo + two, sl] = (dq * factor).astype(BF16)
        dqkv_s[width + lo : width + lo + two, sl] = (live.pop(("dk", t)) * factor).astype(BF16)
        dv = live.pop(("dv", t))
        dv = jnp.concatenate([dv[:head, :LANES], dv[head:, LANES:]], axis=0)
        dqkv_s[2 * width + lo : 2 * width + lo + two, sl] = dv.astype(BF16)

    run([backward_prepare, backward_turn, backward_probs, backward_scores, backward_mix, backward_out], BACKWARD)
    dqkv = dqkv_s[...]
    gqkvt_ref[...] += mm(dqkv, n1a[:208, :], NT)
    dn1 = mm(wqkv_ref[...], dqkv)
    dx = (dx1 + norm_back(dn1, xhat1, rstd1, gain1, 0)).astype(BF16)
    for g in range(group):
        dx_ref[g] = dx[:, g * LANES : g * LANES + length]

    @pl.when(step == pl.num_programs(0) - 1)
    def _():
        gqkv_ref[...] = gqkvt_ref[...].T
        rows = [jnp.sum(ln_acc[i].T, 0, keepdims=True) for i in range(4)]
        vec = jnp.concatenate(
            [rows[0], rows[1], gqkv_ref[width : width + 1, :width], gqkv_ref[width : width + 1, 2 * width :],
             go_ref[width : width + 1], rows[2], rows[3], g2_ref[FH : FH + 1], g1_ref[width : width + 1]],
            axis=1,
        )
        shards, _, block_rows, half = packed_ref.shape
        depth = width // shards
        extra = block_rows - depth
        per_vec = vec.shape[1] // shards
        pack_s[...] = jnp.zeros_like(pack_s)
        for w in range(shards):
            r = slice(w * depth, (w + 1) * depth)
            pack_s[w, :depth, : 4 * width] = jnp.concatenate([gqkv_ref[r, :], go_ref[r, :]], axis=1)
            pack_s[w, :depth, 4 * width :] = g1_ref[r, :]
            at = 4 * w * extra
            pack_s[w, depth:, : 4 * width] = jnp.concatenate(
                [g2_ref[at + j * extra : at + (j + 1) * extra, :] for j in range(4)], axis=1
            )
            pack_s[w, depth : depth + 1, 4 * width : 4 * width + per_vec] = vec[:, w * per_vec : (w + 1) * per_vec]
        for j in range(2):
            packed_ref[:, j] = pack_s[:, :, j * half : (j + 1) * half].astype(BF16)


def run_layer(x, mask, dout, full, group):
    samples, width, length = x.shape
    tokens = group * LANES
    whole = lambda a: pl.BlockSpec(a.shape, lambda i: (0,) * a.ndim)
    per = pl.BlockSpec((group, width, length), lambda i: (i, 0, 0))
    return pl.pallas_call(
        functools.partial(layer_kernel, group),
        grid=(samples // group,),
        in_specs=[per, whole(mask), per, whole(full)],
        out_specs=[per, per, whole(full)],
        out_shape=[jax.ShapeDtypeStruct(x.shape, BF16)] * 2 + [jax.ShapeDtypeStruct(full.shape, BF16)],
        scratch_shapes=[
            pltpu.VMEM((width, 4 * width + 2 * FH), F32),
            pltpu.VMEM((FH, width), F32),
            pltpu.VMEM((1, 8 * width + 2 * FH), F32),
            pltpu.VMEM((width, 3 * width), BF16),
            pltpu.VMEM((width, width), BF16),
            pltpu.VMEM((width, 2 * FH), BF16),
            pltpu.VMEM((FH, width), BF16),
            pltpu.VMEM((3 * width, 256), BF16),
            pltpu.VMEM((width, 256), BF16),
            pltpu.VMEM((2 * FH, 256), BF16),
            pltpu.VMEM((width, FH), BF16),
            pltpu.VMEM((5, width, LANES), F32),
            pltpu.VMEM((256, tokens), BF16),
            pltpu.VMEM((256, tokens), BF16),
            pltpu.VMEM((256, tokens), BF16),
            pltpu.VMEM((272, tokens), BF16),
            pltpu.VMEM((group, H // 2, LANES, 2 * LANES), BF16),
            pltpu.VMEM((208, 3 * width), F32),
            pltpu.VMEM((208, width), F32),
            pltpu.VMEM((208, 2 * FH), F32),
            pltpu.VMEM((272, width), F32),
            pltpu.VMEM((4, width, LANES), F32),
            pltpu.VMEM((full.shape[0], full.shape[2], 2 * full.shape[3]), F32),
            pltpu.VMEM((3 * width, 208), F32),
            pltpu.VMEM((group, H // 2, 64, 2 * LANES), BF16),
            pltpu.VMEM((group, H // 2, 64, LANES), BF16),
            pltpu.VMEM((group, H // 2, 64, LANES), BF16),
            pltpu.VMEM((group, H // 2, 64, 2 * LANES), BF16),
            pltpu.VMEM((group, H // 2, LANES, 2 * LANES), BF16),
            pltpu.VMEM((3 * width, tokens), BF16),
            pltpu.VMEM((width, tokens), F32),
            pltpu.VMEM((group, H // 2, 2 * LANES), F32),
            pltpu.VMEM((group, H // 2, LANES, 2 * LANES), BF16),
        ],
        compiler_params=pltpu.CompilerParams(vmem_limit_bytes=60 * 1024 * 1024),
        name="layer",
    )(x, mask, dout, full)


def send(src, dst, send_sem, recv_sem, device):
    copy = pltpu.make_async_remote_copy(
        src_ref=src, dst_ref=dst, send_sem=send_sem, recv_sem=recv_sem,
        device_id=device, device_id_type=pl.DeviceIdType.MESH,
    )
    copy.start()
    return copy


def hail(devices):
    barrier = pltpu.get_barrier_semaphore()
    for device in devices:
        pl.semaphore_signal(barrier, inc=1, device_id=device, device_id_type=pl.DeviceIdType.MESH)


def places(n, copies_of):
    me, mine = lax.axis_index("wide"), lax.axis_index("narrow")
    core, chip, chips = lax.rem(me, 2), lax.div(me, 2), n // 2
    peer = lambda k: 2 * lax.bitwise_xor(chip, k) + core
    half = lax.rem(mine, 2)
    sibling = {"wide": me + 1 - 2 * core}
    twin = {"narrow": mine + 1 - 2 * half}
    return me, mine, core, chips, peer, half, sibling, twin


def gather_kernel(n, copies_of, attn_hbm, w1_hbm, w2_hbm, vec_hbm, out_ref, attn_ref, w1_ref, w2_ref, vec_ref, load,
                  send1, recv1, send2, recv2, send3, recv3, send4, recv4):
    me, mine, core, chips, peer, half, sibling, twin = places(n, copies_of)
    met = [{"wide": peer(k)} for k in range(1, chips)] + [sibling, twin]
    hail(met)
    pairs = ((attn_hbm, attn_ref), (w1_hbm, w1_ref), (w2_hbm, w2_ref), (vec_hbm, vec_ref))
    loads = [pltpu.make_async_copy(a, b, load.at[i]) for i, (a, b) in enumerate(pairs)]
    for copy in loads:
        copy.start()
    for copy in loads:
        copy.wait()
    width = attn_ref.shape[2]
    extra = w2_ref.shape[0] // 4
    lanes = out_ref.shape[3]
    top = jnp.concatenate([attn_ref[:, i, :] for i in range(4)] + [w1_ref[...]], axis=1)
    bottom = jnp.concatenate(
        [w2_ref[j * extra : (j + 1) * extra, :] for j in range(4)]
        + [jnp.broadcast_to(vec_ref[...], (extra, vec_ref.shape[1])),
           jnp.zeros((extra, 2 * lanes - 4 * width - vec_ref.shape[1]), F32)],
        axis=1,
    )
    block = jnp.concatenate([top, bottom], axis=0).astype(BF16)
    out_ref[me, 0] = block[:, :lanes]
    out_ref[me, 1] = block[:, lanes:]
    pl.semaphore_wait(pltpu.get_barrier_semaphore(), len(met))
    own = out_ref.at[me, half]
    copies = {}
    for k in reversed(range(1, chips)):
        copies[k] = send(own, own, send1.at[k], recv1.at[k], {"wide": peer(k)})
    whole = out_ref.at[me]
    passed = [send(whole, whole, send2.at[0], recv2.at[0], sibling)]
    crossed = {}
    for k in range(1, chips):
        copies[k].wait_recv()
        got = out_ref.at[peer(k), half]
        crossed[k] = send(got, got, send3.at[k], recv3.at[k], twin)
        passed.append(send(got, got, send2.at[k], recv2.at[k], sibling))
    for k in range(1, chips):
        crossed[k].wait_recv()
        got = out_ref.at[peer(k), 1 - half]
        passed.append(send(got, got, send4.at[k], recv4.at[k], sibling))
    for copy in list(copies.values()) + list(crossed.values()):
        copy.wait_send()
    for copy in passed:
        copy.wait()


def gather(attn, w1, w2, vec, n, copies_of):
    rows = attn.shape[0] + w2.shape[0] // 4
    lanes = 4 * attn.shape[2] + w1.shape[1]
    sems = pltpu.SemaphoreType.DMA((n // 2,))
    return pl.pallas_call(
        functools.partial(gather_kernel, n, copies_of),
        out_shape=jax.ShapeDtypeStruct((n, 2, rows, lanes // 2), BF16),
        in_specs=[pl.BlockSpec(memory_space=pl.ANY)] * 4,
        out_specs=pl.BlockSpec(memory_space=pltpu.VMEM),
        scratch_shapes=[pltpu.VMEM(a.shape, F32) for a in (attn, w1, w2, vec)]
        + [pltpu.SemaphoreType.DMA((4,))] + [sems] * 8,
        compiler_params=pltpu.CompilerParams(collective_id=0, has_side_effects=True),
        name="gather",
    )(attn, w1, w2, vec)


def reduce_kernel(n, copies_of, part_hbm, out_ref, part_ref, core_buf, keep_buf, turn_buf, twin_buf, sum_buf,
                  wide_buf, narrow_buf, load, send0, recv0, send1, recv1, send2, recv2, send3, recv3):
    me, mine, core, chips, peer, half, sibling, twin = places(n, copies_of)
    others = [{"narrow": lax.rem(mine + j, copies_of)} for j in range(1, copies_of)]
    met = [{"wide": peer(k)} for k in range(1, chips)] + [sibling] + others
    hail(met)
    mine_parts = pltpu.make_async_copy(part_hbm, part_ref, load)
    mine_parts.start()
    mine_parts.wait()
    pl.semaphore_wait(pltpu.get_barrier_semaphore(), len(met))
    order = list(reversed(range(chips)))
    first, second, third = {}, {}, {}
    for k in order:
        first[k] = send(part_ref.at[peer(k) + 1 - 2 * core], core_buf.at[k], send0.at[k], recv0.at[k], sibling)
    for k in order:
        first[k].wait_recv()
        turn_buf[k] = (part_ref[peer(k), 1 - half].astype(F32) + core_buf[k, 1 - half].astype(F32)).astype(BF16)
        second[k] = send(turn_buf.at[k], twin_buf.at[k], send1.at[k], recv1.at[k], twin)
        keep_buf[k] = part_ref[peer(k), half].astype(F32) + core_buf[k, half].astype(F32)
    for k in order:
        second[k].wait_recv()
        total = keep_buf[k] + twin_buf[k].astype(F32)
        if k:
            sum_buf[k] = total.astype(BF16)
            third[k] = send(sum_buf.at[k], wide_buf.at[k], send2.at[k], recv2.at[k], {"wide": peer(k)})
    for k in range(1, chips):
        third[k].wait_recv()
        total = total + wide_buf[k].astype(F32)
    narrow_buf[mine] = total
    slot = narrow_buf.at[mine]
    fourth = [send(slot, slot, send3.at[j], recv3.at[j], other) for j, other in enumerate(others)]
    for copy in fourth:
        copy.wait_recv()
    lanes = total.shape[1]
    for h in range(2):
        result = narrow_buf[h]
        for j in range(h + 2, copies_of, 2):
            result = result + narrow_buf[j]
        out_ref[:, h * lanes : (h + 1) * lanes] = result
    for copy in list(first.values()) + list(second.values()) + list(third.values()) + fourth:
        copy.wait_send()


def reduce_shares(packed, n, copies_of):
    chips = n // 2
    rows, lanes = packed.shape[2:]
    sems = pltpu.SemaphoreType.DMA((chips,))
    few = pltpu.SemaphoreType.DMA((copies_of,))
    part = lambda kind: pltpu.VMEM((chips, rows, lanes), kind)
    return pl.pallas_call(
        functools.partial(reduce_kernel, n, copies_of),
        out_shape=jax.ShapeDtypeStruct((rows, 2 * lanes), F32),
        in_specs=[pl.BlockSpec(memory_space=pl.ANY)],
        out_specs=pl.BlockSpec(memory_space=pltpu.VMEM),
        scratch_shapes=[pltpu.VMEM(packed.shape, BF16), pltpu.VMEM((chips, 2, rows, lanes), BF16), part(F32),
                        part(BF16), part(BF16), part(BF16), part(BF16), pltpu.VMEM((copies_of, rows, lanes), F32),
                        pltpu.SemaphoreType.DMA] + [sems] * 6 + [few] * 2,
        compiler_params=pltpu.CompilerParams(collective_id=1, has_side_effects=True),
        name="reduce",
    )(packed)


def adamw(weight, first_m, second_m, grad, decay):
    new_m = 0.9 * first_m + 0.1 * grad
    new_v = 0.999 * second_m + 0.001 * grad * grad
    ratio = new_m / (1.0 - 0.9**STEP) / (jnp.sqrt(new_v / (1.0 - 0.999**STEP)) + 1e-08)
    return (weight - 0.1 * (ratio + decay * weight), new_m, new_v)


def update_kernel(grad_ref, *refs):
    ins, outs = refs[:12], refs[12:]
    width = ins[0].shape[2]
    depth = ins[0].shape[0]
    extra = ins[6].shape[0] // 4

    def step(base, index, grad, decay):
        for ref, value in zip(outs[base : base + 3], adamw(*(r[index] for r in ins[base : base + 3]), grad, decay)):
            ref[index] = value

    for i in range(4):
        step(0, (slice(None), i, slice(None)), grad_ref[:depth, i * width : (i + 1) * width], 0.01)
    step(3, (slice(None), slice(None)), grad_ref[:depth, 4 * width :], 0.01)
    for j in range(4):
        step(6, (slice(j * extra, (j + 1) * extra), slice(None)), grad_ref[depth:, j * width : (j + 1) * width], 0.01)
    per_vec = ins[9].shape[1]
    step(9, (slice(None), slice(None)), grad_ref[depth : depth + 1, 4 * width : 4 * width + per_vec], 0.0)


def update(grad, states):
    vmem = pl.BlockSpec(memory_space=pltpu.VMEM)
    return pl.pallas_call(
        update_kernel,
        out_shape=[jax.ShapeDtypeStruct(a.shape, F32) for a in states],
        in_specs=[vmem] * 13,
        out_specs=[vmem] * 12,
        name="update",
    )(grad, *states)


def on_device(layer_input, mask, dout, attn_w, ffn_in, ffn_out, vec,
              m_attn, v_attn, m_in, v_in, m_out, v_out, m_vec, v_vec):
    n, copies_of = lax.axis_size("wide"), lax.axis_size("narrow")
    turn = lambda a: a.transpose(1, 0, 2)
    row = lambda a: a.reshape(1, -1)
    full = gather(turn(attn_w), ffn_in, ffn_out, row(vec), n, copies_of)
    y, dx, packed = run_layer(layer_input.transpose(0, 2, 1), mask, dout.transpose(0, 2, 1), full, GROUP)
    share = reduce_shares(packed, n, copies_of)
    new = update(share, [turn(attn_w), turn(m_attn), turn(v_attn), ffn_in, m_in, v_in, ffn_out, m_out, v_out,
                         row(vec), row(m_vec), row(v_vec)])
    return (y.transpose(0, 2, 1), dx.transpose(0, 2, 1), *(turn(a) for a in new[:3]), *new[3:9],
            *(a.reshape(-1) for a in new[9:]))


def solution(mesh):
    rows = P(("wide", "narrow"), None, None)
    states = [P(None, "wide", None), P("wide", None), P("wide", None), P("wide")]
    moments = [s for s in states for _ in range(2)]
    results = [s for s in states for _ in range(3)]
    return jax.shard_map(
        on_device,
        mesh=mesh,
        in_specs=tuple([rows, P(("wide", "narrow"), None), rows] + states + moments),
        out_specs=tuple([rows, rows] + results),
        check_vma=False,
    )
```

```python
import functools
import jax
import jax.numpy as jnp
from jax import lax
from jax.experimental import pallas as pl
from jax.experimental.pallas import tpu as pltpu
from jax.sharding import PartitionSpec as P

H = 8
FH = 256
STEP = 10
LANES = 128
FORWARD = (0, 1, 7, 8, 9, 12)
BACKWARD = (0, 1, 1, 5, 6, 9)
GROUP = 16
F32 = jnp.float32
BF16 = jnp.bfloat16
NN = (((1,), (0,)), ((), ()))
NT = (((1,), (1,)), ((), ()))


def mm(a, b, dims=NN):
    return lax.dot_general(a, b, dims, preferred_element_type=F32)


def layer_kernel(
    group,
    x_ref, mask_ref, g_ref, full_ref,
    y_ref, dx_ref, packed_ref,
    big, w2f, vec_s, wqkv_ref, wo_ref, w1_ref, w2_ref,
    wqkvt, wot, w1t, w2t, cols, n1a, n2a, oa, ha, e_s,
    gqkv_ref, go_ref, g1_ref, g2_ref, ln_acc, pack_s, gqkvt_ref, g1t_ref,
    q_s, k_s, v_s, d_s, c_s, dqkv_s, o_s, inv_s, et_s,
):
    step = pl.program_id(0)
    length = x_ref.shape[2]
    width = x_ref.shape[1]
    head = width // H
    tokens = group * LANES
    factor = float(head) ** (-0.5)
    log2e = 1.4426950408889634

    @pl.when(step == 0)
    def _():
        shards, _, block_rows, _ = full_ref.shape
        depth = width // shards
        extra = block_rows - depth
        per_vec = vec_s.shape[1] // shards
        for w in range(shards):
            block = jnp.concatenate([full_ref[w, 0], full_ref[w, 1]], axis=1).astype(F32)
            big[w * depth : (w + 1) * depth, :] = block[:depth]
            for j in range(4):
                at = (4 * w + j) * extra
                w2f[at : at + extra, :] = block[depth:, j * width : (j + 1) * width]
            vec_s[:, w * per_vec : (w + 1) * per_vec] = block[depth : depth + 1, 4 * width : 4 * width + per_vec]
        wqkv_ref[...] = big[:, : 3 * width].astype(BF16)
        wo_ref[...] = big[:, 3 * width : 4 * width].astype(BF16)
        w1_ref[...] = big[:, 4 * width :].astype(BF16)
        w2_ref[...] = w2f[...].astype(BF16)

        def aug(w, bias):
            rows = lax.broadcasted_iota(jnp.int32, (64, w.shape[1]), 0)
            tail = jnp.where(rows == 0, jnp.broadcast_to(bias, (64, w.shape[1])), 0.0)
            return jnp.concatenate([w.astype(F32), tail], axis=0).T.astype(BF16)

        zero_row = jnp.zeros((1, width), F32)
        v = vec_s[...]
        piece = lambda i: v[:, i * width : (i + 1) * width]
        bias_qkv = jnp.concatenate([piece(2), zero_row, piece(3)], axis=1)
        wqkvt[...] = aug(wqkv_ref[...], bias_qkv)
        wot[...] = aug(wo_ref[...], piece(4))
        w1t[...] = aug(w1_ref[...], v[:, 8 * width : 8 * width + 2 * FH])
        w2t[...] = w2_ref[...].astype(F32).T.astype(BF16)
        for j, i in enumerate((0, 1, 5, 6, 7)):
            cols[j] = jnp.broadcast_to(piece(i), (LANES, width)).T
        rows = lax.broadcasted_iota(jnp.int32, (64, tokens), 0)
        one = jnp.where(rows == 0, 1.0, 0.0).astype(BF16)
        n1a[width:, :] = one
        n2a[width:, :] = one
        oa[width:, :] = one
        ha[FH:, :] = one[:16]
        gqkvt_ref[...] = jnp.zeros_like(gqkvt_ref)
        go_ref[...] = jnp.zeros_like(go_ref)
        g1t_ref[...] = jnp.zeros_like(g1t_ref)
        g2_ref[...] = jnp.zeros_like(g2_ref)
        ln_acc[...] = jnp.zeros_like(ln_acc)

    def wide(ref, g):
        t = ref[g]
        return jnp.concatenate([t, jnp.zeros((width, LANES - length), t.dtype)], axis=1)

    def tile(col):
        return jnp.concatenate([col] * group, axis=1) if group > 1 else col

    def norm(value):
        center = value - jnp.sum(value, 0, keepdims=True) * (1.0 / width)
        rstd = lax.rsqrt(jnp.sum(center * center, 0, keepdims=True) * (1.0 / width) + 1e-05)
        return center * rstd, rstd

    def norm_back(dn, xhat, rstd, gain, which):
        prod = dn * xhat
        total = ln_acc[which]
        for g in range(dn.shape[1] // LANES):
            total = total + prod[:, g * LANES : (g + 1) * LANES]
        ln_acc[which] = total
        t = dn * gain
        m1 = jnp.sum(t, 0, keepdims=True) * (1.0 / width)
        m2 = jnp.sum(t * xhat, 0, keepdims=True) * (1.0 / width)
        return rstd * (t - m1 - xhat * m2)

    gain1, bias1, gain2, bias2, bias_c2 = (tile(cols[j]) for j in range(5))

    x = jnp.concatenate([wide(x_ref, g) for g in range(group)], axis=1).astype(F32)
    xhat1, rstd1 = norm(x)
    n1a[:width, :] = (xhat1 * gain1 + bias1).astype(BF16)
    qkv = mm(wqkvt[...], n1a[...])

    sub = lax.broadcasted_iota(jnp.int32, (16, LANES), 0)
    lane = lax.broadcasted_iota(jnp.int32, (16, LANES), 1)
    ones_q = jnp.where(sub == 0, 1.0, 0.0)
    ones_v = jnp.where(sub < 2, 1.0, 0.0)
    empty = jnp.zeros((head, LANES), F32)
    two = 2 * head
    live = {}

    def block_diag(first, second, tail_first, tail_second):
        left = jnp.concatenate([first, empty, tail_first], axis=0).astype(BF16)
        right = jnp.concatenate([empty, second, tail_second], axis=0).astype(BF16)
        return jnp.concatenate([left, right], axis=1)

    def run(stages, lags):
        items = [(g, p) for g in range(group) for p in range(H // 2)]
        for t in range(len(items) + max(lags)):
            for stage, lag in reversed(list(zip(stages, lags))):
                if 0 <= t - lag < len(items):
                    stage(t - lag, *items[t - lag])

    def forward_prepare(t, g, p):
        sl = slice(g * LANES, (g + 1) * LANES)
        m = mask_ref[pl.ds(step * group + g, 1), :]
        m = jnp.concatenate([m, jnp.zeros((1, LANES - length), jnp.int32)], axis=1)
        ok = (jnp.broadcast_to(m, (16, LANES)) != 0) | (lane == 0)
        tail_k = jnp.where((sub == 0) & jnp.logical_not(ok), -1e30, 0.0)
        lo = p * two
        q_s[g, p] = block_diag(qkv[lo : lo + head, sl], qkv[lo + head : lo + two, sl], ones_q, ones_q)
        kp = jnp.concatenate([qkv[width + lo : width + lo + two, sl], tail_k], axis=0).astype(BF16)
        k_s[g, p] = kp
        v_s[g, p] = jnp.concatenate([qkv[2 * width + lo : 2 * width + lo + two, sl], ones_v], axis=0).astype(BF16)
        live["k", t] = kp.T

    def forward_scores(t, g, p):
        live["s", t] = mm(live.pop(("k", t)), q_s[g, p])

    def forward_top(t, g, p):
        live["m", t] = jnp.max(live["s", t], 0, keepdims=True)

    def forward_exp(t, g, p):
        e_s[g, p] = jnp.exp2((live.pop(("s", t)) - live.pop(("m", t))) * (factor * log2e)).astype(BF16)

    def forward_mix(t, g, p):
        live["n", t] = mm(v_s[g, p], e_s[g, p])

    def forward_out(t, g, p):
        num = live.pop(("n", t))
        inv = 1.0 / num[two : two + 1]
        inv_s[g, p : p + 1, :] = inv
        sl = slice(g * LANES, (g + 1) * LANES)
        lo = p * two
        o_s[lo : lo + head, sl] = num[:head, :LANES] * inv[:, :LANES]
        o_s[lo + head : lo + two, sl] = num[head:two, LANES:] * inv[:, LANES:]

    run([forward_prepare, forward_scores, forward_top, forward_exp, forward_mix, forward_out], FORWARD)
    oa[:width, :] = o_s[...].astype(BF16)
    x1 = x + mm(wot[...], oa[...])
    xhat2, rstd2 = norm(x1)
    n2a[:width, :] = (xhat2 * gain2 + bias2).astype(BF16)
    gt = jnp.concatenate([wide(g_ref, g) for g in range(group)], axis=1)
    dz_tiles = []
    for t in range(tokens // 256):
        sl = slice(t * 256, (t + 1) * 256)
        z = mm(w1t[...], n2a[:, sl])
        dh = mm(w2_ref[...], gt[:, sl])
        das, dbs = [], []
        for c in range(FH // 64):
            part_a, part_b = z[c * 64 : (c + 1) * 64], z[FH + c * 64 : FH + (c + 1) * 64]
            grad = dh[c * 64 : (c + 1) * 64]
            sigm = 1.0 / (1.0 + jnp.exp2(part_b * -log2e))
            silu = part_b * sigm
            ha[c * 64 : (c + 1) * 64, sl] = (part_a * silu).astype(BF16)
            das.append((grad * silu).astype(BF16))
            dbs.append((grad * part_a * (sigm + silu * (1.0 - sigm))).astype(BF16))
        dz_tiles.append(jnp.concatenate(das + dbs, axis=0))
    dz = jnp.concatenate(dz_tiles, axis=1)
    g2_ref[...] += mm(ha[...], gt, NT)
    g1t_ref[...] += mm(dz, n2a[:208, :], NT)
    dn2 = mm(w1_ref[...], dz)
    dx1 = gt.astype(F32) + norm_back(dn2, xhat2, rstd2, gain2, 1)
    da1 = dx1.astype(BF16)
    go_ref[...] += mm(oa[:208, :], da1, NT)
    do = mm(wo_ref[...], da1).astype(BF16).astype(F32)
    y = (x1 + mm(w2t[...], ha[:FH, :]) + bias_c2).astype(BF16)
    for g in range(group):
        y_ref[g] = y[:, g * LANES : g * LANES + length]

    def backward_prepare(t, g, p):
        sl = slice(g * LANES, (g + 1) * LANES)
        rows, tails = [], []
        for j in range(2):
            r = slice(p * two + j * head, p * two + (j + 1) * head)
            d = do[r, sl]
            inv = inv_s[g, p : p + 1, j * LANES : (j + 1) * LANES]
            low = jnp.sum(d * o_s[r, sl], 0, keepdims=True) * -inv
            hi = low.astype(BF16).astype(F32)
            rows.append(d * inv)
            tails.append(jnp.where(sub == 0, hi, jnp.where(sub == 1, low - hi, 0.0)))
        d_s[g, p] = block_diag(*rows, *tails)
        live["v", t] = v_s[g, p].T
        live["r", t] = jnp.concatenate(rows, axis=0).astype(BF16)

    def backward_probs(t, g, p):
        live["p", t] = mm(live.pop(("v", t)), d_s[g, p])

    def backward_scores(t, g, p):
        c_s[g, p] = (e_s[g, p].astype(F32) * live.pop(("p", t))).astype(BF16)

    def backward_turn(t, g, p):
        e = e_s[g, p]
        et_s[g, p] = jnp.concatenate([e[:, :LANES].T, e[:, LANES:].T], axis=1)

    def backward_mix(t, g, p):
        live["dv", t] = mm(live.pop(("r", t)), et_s[g, p])
        live["dk", t] = mm(q_s[g, p, :two], c_s[g, p], NT)
        live["dq", t] = mm(k_s[g, p, :two], c_s[g, p])

    def backward_out(t, g, p):
        sl = slice(g * LANES, (g + 1) * LANES)
        lo = p * two
        dq = live.pop(("dq", t))
        dq = jnp.concatenate([dq[:head, :LANES], dq[head:, LANES:]], axis=0)
        dqkv_s[lo : lo + two, sl] = (dq * factor).astype(BF16)
        dqkv_s[width + lo : width + lo + two, sl] = (live.pop(("dk", t)) * factor).astype(BF16)
        dv = live.pop(("dv", t))
        dv = jnp.concatenate([dv[:head, :LANES], dv[head:, LANES:]], axis=0)
        dqkv_s[2 * width + lo : 2 * width + lo + two, sl] = dv.astype(BF16)

    run([backward_prepare, backward_turn, backward_probs, backward_scores, backward_mix, backward_out], BACKWARD)
    dqkv = dqkv_s[...]
    gqkvt_ref[...] += mm(dqkv, n1a[:208, :], NT)
    dn1 = mm(wqkv_ref[...], dqkv)
    dx = (dx1 + norm_back(dn1, xhat1, rstd1, gain1, 0)).astype(BF16)
    for g in range(group):
        dx_ref[g] = dx[:, g * LANES : g * LANES + length]

    @pl.when(step == pl.num_programs(0) - 1)
    def _():
        gqkv_ref[...] = gqkvt_ref[...].T
        g1_ref[...] = g1t_ref[...].T
        gains = [jnp.sum(ln_acc[i].T, 0, keepdims=True) for i in range(2)]

        def through(weights, sums):
            return jnp.sum(weights[:, :width].astype(F32) * sums[:, width : width + 1], 0, keepdims=True)

        rows = [gains[0], through(wqkvt, gqkvt_ref), gains[1], through(w1t, g1t_ref)]
        vec = jnp.concatenate(
            [rows[0], rows[1], gqkv_ref[width : width + 1, :width], gqkv_ref[width : width + 1, 2 * width :],
             go_ref[width : width + 1], rows[2], rows[3], g2_ref[FH : FH + 1], g1_ref[width : width + 1]],
            axis=1,
        )
        shards, _, block_rows, half = packed_ref.shape
        depth = width // shards
        extra = block_rows - depth
        per_vec = vec.shape[1] // shards
        pack_s[...] = jnp.zeros_like(pack_s)
        for w in range(shards):
            r = slice(w * depth, (w + 1) * depth)
            pack_s[w, :depth, : 4 * width] = jnp.concatenate([gqkv_ref[r, :], go_ref[r, :]], axis=1)
            pack_s[w, :depth, 4 * width :] = g1_ref[r, :]
            at = 4 * w * extra
            pack_s[w, depth:, : 4 * width] = jnp.concatenate(
                [g2_ref[at + j * extra : at + (j + 1) * extra, :] for j in range(4)], axis=1
            )
            pack_s[w, depth : depth + 1, 4 * width : 4 * width + per_vec] = vec[:, w * per_vec : (w + 1) * per_vec]
        for j in range(2):
            packed_ref[:, j] = pack_s[:, :, j * half : (j + 1) * half].astype(BF16)


def run_layer(x, mask, dout, full, group):
    samples, width, length = x.shape
    tokens = group * LANES
    whole = lambda a: pl.BlockSpec(a.shape, lambda i: (0,) * a.ndim)
    per = pl.BlockSpec((group, width, length), lambda i: (i, 0, 0))
    return pl.pallas_call(
        functools.partial(layer_kernel, group),
        grid=(samples // group,),
        in_specs=[per, whole(mask), per, whole(full)],
        out_specs=[per, per, whole(full)],
        out_shape=[jax.ShapeDtypeStruct(x.shape, BF16)] * 2 + [jax.ShapeDtypeStruct(full.shape, BF16)],
        scratch_shapes=[
            pltpu.VMEM((width, 4 * width + 2 * FH), F32),
            pltpu.VMEM((FH, width), F32),
            pltpu.VMEM((1, 8 * width + 2 * FH), F32),
            pltpu.VMEM((width, 3 * width), BF16),
            pltpu.VMEM((width, width), BF16),
            pltpu.VMEM((width, 2 * FH), BF16),
            pltpu.VMEM((FH, width), BF16),
            pltpu.VMEM((3 * width, 256), BF16),
            pltpu.VMEM((width, 256), BF16),
            pltpu.VMEM((2 * FH, 256), BF16),
            pltpu.VMEM((width, FH), BF16),
            pltpu.VMEM((5, width, LANES), F32),
            pltpu.VMEM((256, tokens), BF16),
            pltpu.VMEM((256, tokens), BF16),
            pltpu.VMEM((256, tokens), BF16),
            pltpu.VMEM((272, tokens), BF16),
            pltpu.VMEM((group, H // 2, LANES, 2 * LANES), BF16),
            pltpu.VMEM((208, 3 * width), F32),
            pltpu.VMEM((208, width), F32),
            pltpu.VMEM((208, 2 * FH), F32),
            pltpu.VMEM((272, width), F32),
            pltpu.VMEM((2, width, LANES), F32),
            pltpu.VMEM((full.shape[0], full.shape[2], 2 * full.shape[3]), F32),
            pltpu.VMEM((3 * width, 208), F32),
            pltpu.VMEM((2 * FH, 208), F32),
            pltpu.VMEM((group, H // 2, 64, 2 * LANES), BF16),
            pltpu.VMEM((group, H // 2, 64, LANES), BF16),
            pltpu.VMEM((group, H // 2, 64, LANES), BF16),
            pltpu.VMEM((group, H // 2, 64, 2 * LANES), BF16),
            pltpu.VMEM((group, H // 2, LANES, 2 * LANES), BF16),
            pltpu.VMEM((3 * width, tokens), BF16),
            pltpu.VMEM((width, tokens), F32),
            pltpu.VMEM((group, H // 2, 2 * LANES), F32),
            pltpu.VMEM((group, H // 2, LANES, 2 * LANES), BF16),
        ],
        compiler_params=pltpu.CompilerParams(vmem_limit_bytes=60 * 1024 * 1024),
        name="layer",
    )(x, mask, dout, full)


def send(src, dst, send_sem, recv_sem, device):
    copy = pltpu.make_async_remote_copy(
        src_ref=src, dst_ref=dst, send_sem=send_sem, recv_sem=recv_sem,
        device_id=device, device_id_type=pl.DeviceIdType.MESH,
    )
    copy.start()
    return copy


def hail(devices):
    barrier = pltpu.get_barrier_semaphore()
    for device in devices:
        pl.semaphore_signal(barrier, inc=1, device_id=device, device_id_type=pl.DeviceIdType.MESH)


def places(n, copies_of):
    me, mine = lax.axis_index("wide"), lax.axis_index("narrow")
    core, chip, chips = lax.rem(me, 2), lax.div(me, 2), n // 2
    peer = lambda k: 2 * lax.bitwise_xor(chip, k) + core
    half = lax.rem(mine, 2)
    sibling = {"wide": me + 1 - 2 * core}
    twin = {"narrow": mine + 1 - 2 * half}
    return me, mine, core, chips, peer, half, sibling, twin


def gather_kernel(n, copies_of, attn_hbm, w1_hbm, w2_hbm, vec_hbm, out_ref, attn_ref, w1_ref, w2_ref, vec_ref, load,
                  send1, recv1, send2, recv2, send3, recv3, send4, recv4):
    me, mine, core, chips, peer, half, sibling, twin = places(n, copies_of)
    met = [{"wide": peer(k)} for k in range(1, chips)] + [sibling, twin]
    hail(met)
    pairs = ((attn_hbm, attn_ref), (w1_hbm, w1_ref), (w2_hbm, w2_ref), (vec_hbm, vec_ref))
    loads = [pltpu.make_async_copy(a, b, load.at[i]) for i, (a, b) in enumerate(pairs)]
    for copy in loads:
        copy.start()
    for copy in loads:
        copy.wait()
    width = attn_ref.shape[2]
    extra = w2_ref.shape[0] // 4
    lanes = out_ref.shape[3]
    top = jnp.concatenate([attn_ref[:, i, :] for i in range(4)] + [w1_ref[...]], axis=1)
    bottom = jnp.concatenate(
        [w2_ref[j * extra : (j + 1) * extra, :] for j in range(4)]
        + [jnp.broadcast_to(vec_ref[...], (extra, vec_ref.shape[1])),
           jnp.zeros((extra, 2 * lanes - 4 * width - vec_ref.shape[1]), F32)],
        axis=1,
    )
    block = jnp.concatenate([top, bottom], axis=0).astype(BF16)
    out_ref[me, 0] = block[:, :lanes]
    out_ref[me, 1] = block[:, lanes:]
    pl.semaphore_wait(pltpu.get_barrier_semaphore(), len(met))
    own = out_ref.at[me, half]
    copies = {}
    for k in reversed(range(1, chips)):
        copies[k] = send(own, own, send1.at[k], recv1.at[k], {"wide": peer(k)})
    whole = out_ref.at[me]
    passed = [send(whole, whole, send2.at[0], recv2.at[0], sibling)]
    crossed = {}
    for k in range(1, chips):
        copies[k].wait_recv()
        got = out_ref.at[peer(k), half]
        crossed[k] = send(got, got, send3.at[k], recv3.at[k], twin)
        passed.append(send(got, got, send2.at[k], recv2.at[k], sibling))
    for k in range(1, chips):
        crossed[k].wait_recv()
        got = out_ref.at[peer(k), 1 - half]
        passed.append(send(got, got, send4.at[k], recv4.at[k], sibling))
    for copy in list(copies.values()) + list(crossed.values()):
        copy.wait_send()
    for copy in passed:
        copy.wait()


def gather(attn, w1, w2, vec, n, copies_of):
    rows = attn.shape[0] + w2.shape[0] // 4
    lanes = 4 * attn.shape[2] + w1.shape[1]
    sems = pltpu.SemaphoreType.DMA((n // 2,))
    return pl.pallas_call(
        functools.partial(gather_kernel, n, copies_of),
        out_shape=jax.ShapeDtypeStruct((n, 2, rows, lanes // 2), BF16),
        in_specs=[pl.BlockSpec(memory_space=pl.ANY)] * 4,
        out_specs=pl.BlockSpec(memory_space=pltpu.VMEM),
        scratch_shapes=[pltpu.VMEM(a.shape, F32) for a in (attn, w1, w2, vec)]
        + [pltpu.SemaphoreType.DMA((4,))] + [sems] * 8,
        compiler_params=pltpu.CompilerParams(collective_id=0, has_side_effects=True),
        name="gather",
    )(attn, w1, w2, vec)


def reduce_kernel(n, copies_of, part_hbm, out_ref, part_ref, core_buf, keep_buf, turn_buf, twin_buf, sum_buf,
                  wide_buf, narrow_buf, load, send0, recv0, send1, recv1, send2, recv2, send3, recv3):
    me, mine, core, chips, peer, half, sibling, twin = places(n, copies_of)
    others = [{"narrow": lax.rem(mine + j, copies_of)} for j in range(1, copies_of)]
    met = [{"wide": peer(k)} for k in range(1, chips)] + [sibling] + others
    hail(met)
    mine_parts = pltpu.make_async_copy(part_hbm, part_ref, load)
    mine_parts.start()
    mine_parts.wait()
    pl.semaphore_wait(pltpu.get_barrier_semaphore(), len(met))
    order = list(reversed(range(chips)))
    first, second, third = {}, {}, {}
    for k in order:
        first[k] = send(part_ref.at[peer(k) + 1 - 2 * core], core_buf.at[k], send0.at[k], recv0.at[k], sibling)
    for k in order:
        first[k].wait_recv()
        turn_buf[k] = (part_ref[peer(k), 1 - half].astype(F32) + core_buf[k, 1 - half].astype(F32)).astype(BF16)
        second[k] = send(turn_buf.at[k], twin_buf.at[k], send1.at[k], recv1.at[k], twin)
        keep_buf[k] = part_ref[peer(k), half].astype(F32) + core_buf[k, half].astype(F32)
    for k in order:
        second[k].wait_recv()
        total = keep_buf[k] + twin_buf[k].astype(F32)
        if k:
            sum_buf[k] = total.astype(BF16)
            third[k] = send(sum_buf.at[k], wide_buf.at[k], send2.at[k], recv2.at[k], {"wide": peer(k)})
    for k in range(1, chips):
        third[k].wait_recv()
        total = total + wide_buf[k].astype(F32)
    narrow_buf[mine] = total
    slot = narrow_buf.at[mine]
    fourth = [send(slot, slot, send3.at[j], recv3.at[j], other) for j, other in enumerate(others)]
    for copy in fourth:
        copy.wait_recv()
    lanes = total.shape[1]
    for h in range(2):
        result = narrow_buf[h]
        for j in range(h + 2, copies_of, 2):
            result = result + narrow_buf[j]
        out_ref[:, h * lanes : (h + 1) * lanes] = result
    for copy in list(first.values()) + list(second.values()) + list(third.values()) + fourth:
        copy.wait_send()


def reduce_shares(packed, n, copies_of):
    chips = n // 2
    rows, lanes = packed.shape[2:]
    sems = pltpu.SemaphoreType.DMA((chips,))
    few = pltpu.SemaphoreType.DMA((copies_of,))
    part = lambda kind: pltpu.VMEM((chips, rows, lanes), kind)
    return pl.pallas_call(
        functools.partial(reduce_kernel, n, copies_of),
        out_shape=jax.ShapeDtypeStruct((rows, 2 * lanes), F32),
        in_specs=[pl.BlockSpec(memory_space=pl.ANY)],
        out_specs=pl.BlockSpec(memory_space=pltpu.VMEM),
        scratch_shapes=[pltpu.VMEM(packed.shape, BF16), pltpu.VMEM((chips, 2, rows, lanes), BF16), part(F32),
                        part(BF16), part(BF16), part(BF16), part(BF16), pltpu.VMEM((copies_of, rows, lanes), F32),
                        pltpu.SemaphoreType.DMA] + [sems] * 6 + [few] * 2,
        compiler_params=pltpu.CompilerParams(collective_id=1, has_side_effects=True, vmem_limit_bytes=56000000),
        name="reduce",
    )(packed)


def adamw(weight, first_m, second_m, grad, decay):
    new_m = 0.9 * first_m + 0.1 * grad
    new_v = 0.999 * second_m + 0.001 * grad * grad
    ratio = new_m / (1.0 - 0.9**STEP) / (jnp.sqrt(new_v / (1.0 - 0.999**STEP)) + 1e-08)
    return (weight - 0.1 * (ratio + decay * weight), new_m, new_v)


def update_kernel(grad_ref, *refs):
    ins, outs = refs[:12], refs[12:]
    width = ins[0].shape[2]
    depth = ins[0].shape[0]
    extra = ins[6].shape[0] // 4

    def step(base, index, grad, decay):
        for ref, value in zip(outs[base : base + 3], adamw(*(r[index] for r in ins[base : base + 3]), grad, decay)):
            ref[index] = value

    for i in range(4):
        step(0, (slice(None), i, slice(None)), grad_ref[:depth, i * width : (i + 1) * width], 0.01)
    step(3, (slice(None), slice(None)), grad_ref[:depth, 4 * width :], 0.01)
    for j in range(4):
        step(6, (slice(j * extra, (j + 1) * extra), slice(None)), grad_ref[depth:, j * width : (j + 1) * width], 0.01)
    per_vec = ins[9].shape[1]
    step(9, (slice(None), slice(None)), grad_ref[depth : depth + 1, 4 * width : 4 * width + per_vec], 0.0)


def update(grad, states):
    vmem = pl.BlockSpec(memory_space=pltpu.VMEM)
    return pl.pallas_call(
        update_kernel,
        out_shape=[jax.ShapeDtypeStruct(a.shape, F32) for a in states],
        in_specs=[vmem] * 13,
        out_specs=[vmem] * 12,
        compiler_params=pltpu.CompilerParams(vmem_limit_bytes=4 * 1024 * 1024),
        name="update",
    )(grad, *states)


def on_device(layer_input, mask, dout, attn_w, ffn_in, ffn_out, vec,
              m_attn, v_attn, m_in, v_in, m_out, v_out, m_vec, v_vec):
    n, copies_of = lax.axis_size("wide"), lax.axis_size("narrow")
    turn = lambda a: a.transpose(1, 0, 2)
    row = lambda a: a.reshape(1, -1)
    full = gather(turn(attn_w), ffn_in, ffn_out, row(vec), n, copies_of)
    y, dx, packed = run_layer(layer_input.transpose(0, 2, 1), mask, dout.transpose(0, 2, 1), full, GROUP)
    share = reduce_shares(packed, n, copies_of)
    new = update(share, [turn(attn_w), turn(m_attn), turn(v_attn), ffn_in, m_in, v_in, ffn_out, m_out, v_out,
                         row(vec), row(m_vec), row(v_vec)])
    return (y.transpose(0, 2, 1), dx.transpose(0, 2, 1), *(turn(a) for a in new[:3]), *new[3:9],
            *(a.reshape(-1) for a in new[9:]))


def solution(mesh):
    rows = P(("wide", "narrow"), None, None)
    states = [P(None, "wide", None), P("wide", None), P("wide", None), P("wide")]
    moments = [s for s in states for _ in range(2)]
    results = [s for s in states for _ in range(3)]
    return jax.shard_map(
        on_device,
        mesh=mesh,
        in_specs=tuple([rows, P(("wide", "narrow"), None), rows] + states + moments),
        out_specs=tuple([rows, rows] + results),
        check_vma=False,
    )
```

```python
import functools
import jax
import jax.numpy as jnp
from jax import lax
from jax.experimental import pallas as pl
from jax.experimental.pallas import tpu as pltpu
from jax.sharding import PartitionSpec as P

H = 8
FH = 256
STEP = 10
LANES = 128
FORWARD = (0, 1, 7, 8, 9, 12)
BACKWARD = (0, 1, 1, 5, 6, 9)
GROUP = 16
F32 = jnp.float32
BF16 = jnp.bfloat16
NN = (((1,), (0,)), ((), ()))
NT = (((1,), (1,)), ((), ()))


def mm(a, b, dims=NN):
    return lax.dot_general(a, b, dims, preferred_element_type=F32)


def layer_kernel(
    group,
    x_hbm, mask_hbm, g_hbm, full_hbm,
    y_hbm, dx_hbm, packed_ref,
    big, w2f, vec_s, wqkv_ref, wo_ref, w1_ref, w2_ref,
    wqkvt, wot, w1t, w2t, cols, n1a, n2a, oa, ha, e_s,
    gqkv_ref, go_ref, g1_ref, g2_ref, ln_acc, pack_s, gqkvt_ref, g1t_ref,
    q_s, k_s, v_s, d_s, c_s, dqkv_s, o_s, inv_s, et_s,
    full_ref, mask_ref, x_b, g_b, y_b, dx_b, once_sem, in_sem, out_sem,
):
    step = pl.program_id(0)
    length = x_hbm.shape[2]
    width = x_hbm.shape[1]
    slot = lax.rem(step, 2)
    steps = x_hbm.shape[0] // group
    x_ref, g_ref, y_ref, dx_ref = (b.at[slot] for b in (x_b, g_b, y_b, dx_b))

    def arriving(index):
        into = lax.rem(index, 2)
        rows = pl.ds(index * group, group)
        return [
            pltpu.make_async_copy(x_hbm.at[rows], x_b.at[into], in_sem.at[0, into]),
            pltpu.make_async_copy(g_hbm.at[rows], g_b.at[into], in_sem.at[1, into]),
        ]

    def leaving(index):
        out_of = lax.rem(index, 2)
        rows = pl.ds(index * group, group)
        return [
            pltpu.make_async_copy(y_b.at[out_of], y_hbm.at[rows], out_sem.at[0, out_of]),
            pltpu.make_async_copy(dx_b.at[out_of], dx_hbm.at[rows], out_sem.at[1, out_of]),
        ]
    head = width // H
    tokens = group * LANES
    factor = float(head) ** (-0.5)
    log2e = 1.4426950408889634

    @pl.when(step == 0)
    def _():
        first = [
            pltpu.make_async_copy(full_hbm, full_ref, once_sem.at[0]),
            pltpu.make_async_copy(mask_hbm, mask_ref, once_sem.at[1]),
        ]
        for copy in first + arriving(0):
            copy.start()
        for copy in first:
            copy.wait()
        shards, _, block_rows, _ = full_ref.shape
        depth = width // shards
        extra = block_rows - depth
        per_vec = vec_s.shape[1] // shards
        for w in range(shards):
            block = jnp.concatenate([full_ref[w, 0], full_ref[w, 1]], axis=1).astype(F32)
            big[w * depth : (w + 1) * depth, :] = block[:depth]
            for j in range(4):
                at = (4 * w + j) * extra
                w2f[at : at + extra, :] = block[depth:, j * width : (j + 1) * width]
            vec_s[:, w * per_vec : (w + 1) * per_vec] = block[depth : depth + 1, 4 * width : 4 * width + per_vec]
        wqkv_ref[...] = big[:, : 3 * width].astype(BF16)
        wo_ref[...] = big[:, 3 * width : 4 * width].astype(BF16)
        w1_ref[...] = big[:, 4 * width :].astype(BF16)
        w2_ref[...] = w2f[...].astype(BF16)

        def aug(w, bias):
            rows = lax.broadcasted_iota(jnp.int32, (64, w.shape[1]), 0)
            tail = jnp.where(rows == 0, jnp.broadcast_to(bias, (64, w.shape[1])), 0.0)
            return jnp.concatenate([w.astype(F32), tail], axis=0).T.astype(BF16)

        zero_row = jnp.zeros((1, width), F32)
        v = vec_s[...]
        piece = lambda i: v[:, i * width : (i + 1) * width]
        bias_qkv = jnp.concatenate([piece(2), zero_row, piece(3)], axis=1)
        wqkvt[...] = aug(wqkv_ref[...], bias_qkv)
        wot[...] = aug(wo_ref[...], piece(4))
        w1t[...] = aug(w1_ref[...], v[:, 8 * width : 8 * width + 2 * FH])
        w2t[...] = w2_ref[...].astype(F32).T.astype(BF16)
        for j, i in enumerate((0, 1, 5, 6, 7)):
            cols[j] = jnp.broadcast_to(piece(i), (LANES, width)).T
        rows = lax.broadcasted_iota(jnp.int32, (64, tokens), 0)
        one = jnp.where(rows == 0, 1.0, 0.0).astype(BF16)
        n1a[width:, :] = one
        n2a[width:, :] = one
        oa[width:, :] = one
        ha[FH:, :] = one[:16]
        gqkvt_ref[...] = jnp.zeros_like(gqkvt_ref)
        go_ref[...] = jnp.zeros_like(go_ref)
        g1t_ref[...] = jnp.zeros_like(g1t_ref)
        g2_ref[...] = jnp.zeros_like(g2_ref)
        ln_acc[...] = jnp.zeros_like(ln_acc)

    @pl.when(step + 1 < pl.num_programs(0))
    def _():
        for copy in arriving(step + 1):
            copy.start()

    for copy in arriving(step):
        copy.wait()

    @pl.when(step > 1)
    def _():
        for copy in leaving(step - 2):
            copy.wait()

    def wide(ref, g):
        t = ref[g]
        return jnp.concatenate([t, jnp.zeros((width, LANES - length), t.dtype)], axis=1)

    def tile(col):
        return jnp.concatenate([col] * group, axis=1) if group > 1 else col

    def norm(value):
        center = value - jnp.sum(value, 0, keepdims=True) * (1.0 / width)
        rstd = lax.rsqrt(jnp.sum(center * center, 0, keepdims=True) * (1.0 / width) + 1e-05)
        return center * rstd, rstd

    def norm_back(dn, xhat, rstd, gain, which):
        prod = dn * xhat
        total = ln_acc[which]
        for g in range(dn.shape[1] // LANES):
            total = total + prod[:, g * LANES : (g + 1) * LANES]
        ln_acc[which] = total
        t = dn * gain
        m1 = jnp.sum(t, 0, keepdims=True) * (1.0 / width)
        m2 = jnp.sum(t * xhat, 0, keepdims=True) * (1.0 / width)
        return rstd * (t - m1 - xhat * m2)

    gain1, bias1, gain2, bias2, bias_c2 = (tile(cols[j]) for j in range(5))

    x = jnp.concatenate([wide(x_ref, g) for g in range(group)], axis=1).astype(F32)
    xhat1, rstd1 = norm(x)
    n1a[:width, :] = (xhat1 * gain1 + bias1).astype(BF16)
    qkv = mm(wqkvt[...], n1a[...])

    sub = lax.broadcasted_iota(jnp.int32, (16, LANES), 0)
    lane = lax.broadcasted_iota(jnp.int32, (16, LANES), 1)
    ones_q = jnp.where(sub == 0, 1.0, 0.0)
    ones_v = jnp.where(sub < 2, 1.0, 0.0)
    empty = jnp.zeros((head, LANES), F32)
    two = 2 * head
    live = {}

    def block_diag(first, second, tail_first, tail_second):
        left = jnp.concatenate([first, empty, tail_first], axis=0).astype(BF16)
        right = jnp.concatenate([empty, second, tail_second], axis=0).astype(BF16)
        return jnp.concatenate([left, right], axis=1)

    def run(stages, lags):
        items = [(g, p) for g in range(group) for p in range(H // 2)]
        for t in range(len(items) + max(lags)):
            for stage, lag in reversed(list(zip(stages, lags))):
                if 0 <= t - lag < len(items):
                    stage(t - lag, *items[t - lag])

    def forward_prepare(t, g, p):
        sl = slice(g * LANES, (g + 1) * LANES)
        m = mask_ref[pl.ds(step * group + g, 1), :]
        m = jnp.concatenate([m, jnp.zeros((1, LANES - length), jnp.int32)], axis=1)
        ok = (jnp.broadcast_to(m, (16, LANES)) != 0) | (lane == 0)
        tail_k = jnp.where((sub == 0) & jnp.logical_not(ok), -1e30, 0.0)
        lo = p * two
        q_s[g, p] = block_diag(qkv[lo : lo + head, sl], qkv[lo + head : lo + two, sl], ones_q, ones_q)
        kp = jnp.concatenate([qkv[width + lo : width + lo + two, sl], tail_k], axis=0).astype(BF16)
        k_s[g, p] = kp
        v_s[g, p] = jnp.concatenate([qkv[2 * width + lo : 2 * width + lo + two, sl], ones_v], axis=0).astype(BF16)
        live["k", t] = kp.T

    def forward_scores(t, g, p):
        live["s", t] = mm(live.pop(("k", t)), q_s[g, p])

    def forward_top(t, g, p):
        live["m", t] = jnp.max(live["s", t], 0, keepdims=True)

    def forward_exp(t, g, p):
        e_s[g, p] = jnp.exp2((live.pop(("s", t)) - live.pop(("m", t))) * (factor * log2e)).astype(BF16)

    def forward_mix(t, g, p):
        live["n", t] = mm(v_s[g, p], e_s[g, p])

    def forward_out(t, g, p):
        num = live.pop(("n", t))
        inv = 1.0 / num[two : two + 1]
        inv_s[g, p : p + 1, :] = inv
        sl = slice(g * LANES, (g + 1) * LANES)
        lo = p * two
        o_s[lo : lo + head, sl] = num[:head, :LANES] * inv[:, :LANES]
        o_s[lo + head : lo + two, sl] = num[head:two, LANES:] * inv[:, LANES:]

    run([forward_prepare, forward_scores, forward_top, forward_exp, forward_mix, forward_out], FORWARD)
    oa[:width, :] = o_s[...].astype(BF16)
    x1 = x + mm(wot[...], oa[...])
    xhat2, rstd2 = norm(x1)
    n2a[:width, :] = (xhat2 * gain2 + bias2).astype(BF16)
    gt = jnp.concatenate([wide(g_ref, g) for g in range(group)], axis=1)
    dz_tiles = []
    for t in range(tokens // 256):
        sl = slice(t * 256, (t + 1) * 256)
        z = mm(w1t[...], n2a[:, sl])
        dh = mm(w2_ref[...], gt[:, sl])
        das, dbs = [], []
        for c in range(FH // 64):
            part_a, part_b = z[c * 64 : (c + 1) * 64], z[FH + c * 64 : FH + (c + 1) * 64]
            grad = dh[c * 64 : (c + 1) * 64]
            sigm = 1.0 / (1.0 + jnp.exp2(part_b * -log2e))
            silu = part_b * sigm
            ha[c * 64 : (c + 1) * 64, sl] = (part_a * silu).astype(BF16)
            das.append((grad * silu).astype(BF16))
            dbs.append((grad * part_a * (sigm + silu * (1.0 - sigm))).astype(BF16))
        dz_tiles.append(jnp.concatenate(das + dbs, axis=0))
    dz = jnp.concatenate(dz_tiles, axis=1)
    g2_ref[...] += mm(ha[...], gt, NT)
    g1t_ref[...] += mm(dz, n2a[:208, :], NT)
    dn2 = mm(w1_ref[...], dz)
    dx1 = gt.astype(F32) + norm_back(dn2, xhat2, rstd2, gain2, 1)
    da1 = dx1.astype(BF16)
    go_ref[...] += mm(oa[:208, :], da1, NT)
    do = mm(wo_ref[...], da1).astype(BF16).astype(F32)
    y = (x1 + mm(w2t[...], ha[:FH, :]) + bias_c2).astype(BF16)
    for g in range(group):
        y_ref[g] = y[:, g * LANES : g * LANES + length]

    def backward_prepare(t, g, p):
        sl = slice(g * LANES, (g + 1) * LANES)
        rows, tails = [], []
        for j in range(2):
            r = slice(p * two + j * head, p * two + (j + 1) * head)
            d = do[r, sl]
            inv = inv_s[g, p : p + 1, j * LANES : (j + 1) * LANES]
            low = jnp.sum(d * o_s[r, sl], 0, keepdims=True) * -inv
            hi = low.astype(BF16).astype(F32)
            rows.append(d * inv)
            tails.append(jnp.where(sub == 0, hi, jnp.where(sub == 1, low - hi, 0.0)))
        d_s[g, p] = block_diag(*rows, *tails)
        live["v", t] = v_s[g, p].T
        live["r", t] = jnp.concatenate(rows, axis=0).astype(BF16)

    def backward_probs(t, g, p):
        live["p", t] = mm(live.pop(("v", t)), d_s[g, p])

    def backward_scores(t, g, p):
        c_s[g, p] = (e_s[g, p].astype(F32) * live.pop(("p", t))).astype(BF16)

    def backward_turn(t, g, p):
        e = e_s[g, p]
        et_s[g, p] = jnp.concatenate([e[:, :LANES].T, e[:, LANES:].T], axis=1)

    def backward_mix(t, g, p):
        live["dv", t] = mm(live.pop(("r", t)), et_s[g, p])
        live["dk", t] = mm(q_s[g, p, :two], c_s[g, p], NT)
        live["dq", t] = mm(k_s[g, p, :two], c_s[g, p])

    def backward_out(t, g, p):
        sl = slice(g * LANES, (g + 1) * LANES)
        lo = p * two
        dq = live.pop(("dq", t))
        dq = jnp.concatenate([dq[:head, :LANES], dq[head:, LANES:]], axis=0)
        dqkv_s[lo : lo + two, sl] = (dq * factor).astype(BF16)
        dqkv_s[width + lo : width + lo + two, sl] = (live.pop(("dk", t)) * factor).astype(BF16)
        dv = live.pop(("dv", t))
        dv = jnp.concatenate([dv[:head, :LANES], dv[head:, LANES:]], axis=0)
        dqkv_s[2 * width + lo : 2 * width + lo + two, sl] = dv.astype(BF16)

    run([backward_prepare, backward_turn, backward_probs, backward_scores, backward_mix, backward_out], BACKWARD)
    dqkv = dqkv_s[...]
    gqkvt_ref[...] += mm(dqkv, n1a[:208, :], NT)
    dn1 = mm(wqkv_ref[...], dqkv)
    dx = (dx1 + norm_back(dn1, xhat1, rstd1, gain1, 0)).astype(BF16)
    for g in range(group):
        dx_ref[g] = dx[:, g * LANES : g * LANES + length]

    for copy in leaving(step):
        copy.start()

    @pl.when(step == pl.num_programs(0) - 1)
    def _():
        gqkv_ref[...] = gqkvt_ref[...].T
        g1_ref[...] = g1t_ref[...].T
        gains = [jnp.sum(ln_acc[i].T, 0, keepdims=True) for i in range(2)]

        def through(weights, sums):
            return jnp.sum(weights[:, :width].astype(F32) * sums[:, width : width + 1], 0, keepdims=True)

        rows = [gains[0], through(wqkvt, gqkvt_ref), gains[1], through(w1t, g1t_ref)]
        vec = jnp.concatenate(
            [rows[0], rows[1], gqkv_ref[width : width + 1, :width], gqkv_ref[width : width + 1, 2 * width :],
             go_ref[width : width + 1], rows[2], rows[3], g2_ref[FH : FH + 1], g1_ref[width : width + 1]],
            axis=1,
        )
        shards, _, block_rows, half = packed_ref.shape
        depth = width // shards
        extra = block_rows - depth
        per_vec = vec.shape[1] // shards
        pack_s[...] = jnp.zeros_like(pack_s)
        for w in range(shards):
            r = slice(w * depth, (w + 1) * depth)
            pack_s[w, :depth, : 4 * width] = jnp.concatenate([gqkv_ref[r, :], go_ref[r, :]], axis=1)
            pack_s[w, :depth, 4 * width :] = g1_ref[r, :]
            at = 4 * w * extra
            pack_s[w, depth:, : 4 * width] = jnp.concatenate(
                [g2_ref[at + j * extra : at + (j + 1) * extra, :] for j in range(4)], axis=1
            )
            pack_s[w, depth : depth + 1, 4 * width : 4 * width + per_vec] = vec[:, w * per_vec : (w + 1) * per_vec]
        for j in range(2):
            packed_ref[:, j] = pack_s[:, :, j * half : (j + 1) * half].astype(BF16)
        for copy in leaving(step) + (leaving(step - 1) if steps > 1 else []):
            copy.wait()


def run_layer(x, mask, dout, full, group):
    samples, width, length = x.shape
    tokens = group * LANES
    whole = lambda a: pl.BlockSpec(a.shape, lambda i: (0,) * a.ndim)
    apart = pl.BlockSpec(memory_space=pl.ANY)
    block = (group, width, length)
    return pl.pallas_call(
        functools.partial(layer_kernel, group),
        grid=(samples // group,),
        in_specs=[apart] * 4,
        out_specs=[apart, apart, whole(full)],
        out_shape=[jax.ShapeDtypeStruct(x.shape, BF16)] * 2 + [jax.ShapeDtypeStruct(full.shape, BF16)],
        scratch_shapes=[
            pltpu.VMEM((width, 4 * width + 2 * FH), F32),
            pltpu.VMEM((FH, width), F32),
            pltpu.VMEM((1, 8 * width + 2 * FH), F32),
            pltpu.VMEM((width, 3 * width), BF16),
            pltpu.VMEM((width, width), BF16),
            pltpu.VMEM((width, 2 * FH), BF16),
            pltpu.VMEM((FH, width), BF16),
            pltpu.VMEM((3 * width, 256), BF16),
            pltpu.VMEM((width, 256), BF16),
            pltpu.VMEM((2 * FH, 256), BF16),
            pltpu.VMEM((width, FH), BF16),
            pltpu.VMEM((5, width, LANES), F32),
            pltpu.VMEM((256, tokens), BF16),
            pltpu.VMEM((256, tokens), BF16),
            pltpu.VMEM((256, tokens), BF16),
            pltpu.VMEM((272, tokens), BF16),
            pltpu.VMEM((group, H // 2, LANES, 2 * LANES), BF16),
            pltpu.VMEM((208, 3 * width), F32),
            pltpu.VMEM((208, width), F32),
            pltpu.VMEM((208, 2 * FH), F32),
            pltpu.VMEM((272, width), F32),
            pltpu.VMEM((2, width, LANES), F32),
            pltpu.VMEM((full.shape[0], full.shape[2], 2 * full.shape[3]), F32),
            pltpu.VMEM((3 * width, 208), F32),
            pltpu.VMEM((2 * FH, 208), F32),
            pltpu.VMEM((group, H // 2, 64, 2 * LANES), BF16),
            pltpu.VMEM((group, H // 2, 64, LANES), BF16),
            pltpu.VMEM((group, H // 2, 64, LANES), BF16),
            pltpu.VMEM((group, H // 2, 64, 2 * LANES), BF16),
            pltpu.VMEM((group, H // 2, LANES, 2 * LANES), BF16),
            pltpu.VMEM((3 * width, tokens), BF16),
            pltpu.VMEM((width, tokens), F32),
            pltpu.VMEM((group, H // 2, 2 * LANES), F32),
            pltpu.VMEM((group, H // 2, LANES, 2 * LANES), BF16),
            pltpu.VMEM(full.shape, BF16),
            pltpu.VMEM(mask.shape, jnp.int32),
            pltpu.VMEM((2,) + block, BF16),
            pltpu.VMEM((2,) + block, BF16),
            pltpu.VMEM((2,) + block, BF16),
            pltpu.VMEM((2,) + block, BF16),
            pltpu.SemaphoreType.DMA((2,)),
            pltpu.SemaphoreType.DMA((2, 2)),
            pltpu.SemaphoreType.DMA((2, 2)),
        ],
        compiler_params=pltpu.CompilerParams(vmem_limit_bytes=60 * 1024 * 1024),
        name="layer",
    )(x, mask, dout, full)


def send(src, dst, send_sem, recv_sem, device):
    copy = pltpu.make_async_remote_copy(
        src_ref=src, dst_ref=dst, send_sem=send_sem, recv_sem=recv_sem,
        device_id=device, device_id_type=pl.DeviceIdType.MESH,
    )
    copy.start()
    return copy


def hail(devices):
    barrier = pltpu.get_barrier_semaphore()
    for device in devices:
        pl.semaphore_signal(barrier, inc=1, device_id=device, device_id_type=pl.DeviceIdType.MESH)


def places(n, copies_of):
    me, mine = lax.axis_index("wide"), lax.axis_index("narrow")
    core, chip, chips = lax.rem(me, 2), lax.div(me, 2), n // 2
    peer = lambda k: 2 * lax.bitwise_xor(chip, k) + core
    half = lax.rem(mine, 2)
    sibling = {"wide": me + 1 - 2 * core}
    twin = {"narrow": mine + 1 - 2 * half}
    return me, mine, core, chips, peer, half, sibling, twin


def gather_kernel(n, copies_of, attn_hbm, w1_hbm, w2_hbm, vec_hbm, out_ref, attn_ref, w1_ref, w2_ref, vec_ref, load,
                  send1, recv1, send2, recv2, send3, recv3, send4, recv4):
    me, mine, core, chips, peer, half, sibling, twin = places(n, copies_of)
    met = [{"wide": peer(k)} for k in range(1, chips)] + [sibling, twin]
    hail(met)
    pairs = ((attn_hbm, attn_ref), (w1_hbm, w1_ref), (w2_hbm, w2_ref), (vec_hbm, vec_ref))
    loads = [pltpu.make_async_copy(a, b, load.at[i]) for i, (a, b) in enumerate(pairs)]
    for copy in loads:
        copy.start()
    for copy in loads:
        copy.wait()
    width = attn_ref.shape[2]
    extra = w2_ref.shape[0] // 4
    lanes = out_ref.shape[3]
    top = jnp.concatenate([attn_ref[:, i, :] for i in range(4)] + [w1_ref[...]], axis=1)
    bottom = jnp.concatenate(
        [w2_ref[j * extra : (j + 1) * extra, :] for j in range(4)]
        + [jnp.broadcast_to(vec_ref[...], (extra, vec_ref.shape[1])),
           jnp.zeros((extra, 2 * lanes - 4 * width - vec_ref.shape[1]), F32)],
        axis=1,
    )
    block = jnp.concatenate([top, bottom], axis=0).astype(BF16)
    out_ref[me, 0] = block[:, :lanes]
    out_ref[me, 1] = block[:, lanes:]
    pl.semaphore_wait(pltpu.get_barrier_semaphore(), len(met))
    own = out_ref.at[me, half]
    copies = {}
    for k in reversed(range(1, chips)):
        copies[k] = send(own, own, send1.at[k], recv1.at[k], {"wide": peer(k)})
    whole = out_ref.at[me]
    passed = [send(whole, whole, send2.at[0], recv2.at[0], sibling)]
    crossed = {}
    for k in range(1, chips):
        copies[k].wait_recv()
        got = out_ref.at[peer(k), half]
        crossed[k] = send(got, got, send3.at[k], recv3.at[k], twin)
        passed.append(send(got, got, send2.at[k], recv2.at[k], sibling))
    for k in range(1, chips):
        crossed[k].wait_recv()
        got = out_ref.at[peer(k), 1 - half]
        passed.append(send(got, got, send4.at[k], recv4.at[k], sibling))
    for copy in list(copies.values()) + list(crossed.values()):
        copy.wait_send()
    for copy in passed:
        copy.wait()


def gather(attn, w1, w2, vec, n, copies_of):
    rows = attn.shape[0] + w2.shape[0] // 4
    lanes = 4 * attn.shape[2] + w1.shape[1]
    sems = pltpu.SemaphoreType.DMA((n // 2,))
    return pl.pallas_call(
        functools.partial(gather_kernel, n, copies_of),
        out_shape=jax.ShapeDtypeStruct((n, 2, rows, lanes // 2), BF16),
        in_specs=[pl.BlockSpec(memory_space=pl.ANY)] * 4,
        out_specs=pl.BlockSpec(memory_space=pltpu.VMEM),
        scratch_shapes=[pltpu.VMEM(a.shape, F32) for a in (attn, w1, w2, vec)]
        + [pltpu.SemaphoreType.DMA((4,))] + [sems] * 8,
        compiler_params=pltpu.CompilerParams(collective_id=0, has_side_effects=True),
        name="gather",
    )(attn, w1, w2, vec)


def reduce_kernel(n, copies_of, part_hbm, out_ref, part_ref, core_buf, keep_buf, turn_buf, twin_buf, sum_buf,
                  wide_buf, narrow_buf, load, send0, recv0, send1, recv1, send2, recv2, send3, recv3):
    me, mine, core, chips, peer, half, sibling, twin = places(n, copies_of)
    others = [{"narrow": lax.rem(mine + j, copies_of)} for j in range(1, copies_of)]
    met = [{"wide": peer(k)} for k in range(1, chips)] + [sibling] + others
    hail(met)
    mine_parts = pltpu.make_async_copy(part_hbm, part_ref, load)
    mine_parts.start()
    mine_parts.wait()
    pl.semaphore_wait(pltpu.get_barrier_semaphore(), len(met))
    order = list(reversed(range(chips)))
    first, second, third = {}, {}, {}
    for k in order:
        first[k] = send(part_ref.at[peer(k) + 1 - 2 * core], core_buf.at[k], send0.at[k], recv0.at[k], sibling)
    for k in order:
        first[k].wait_recv()
        turn_buf[k] = (part_ref[peer(k), 1 - half].astype(F32) + core_buf[k, 1 - half].astype(F32)).astype(BF16)
        second[k] = send(turn_buf.at[k], twin_buf.at[k], send1.at[k], recv1.at[k], twin)
        keep_buf[k] = part_ref[peer(k), half].astype(F32) + core_buf[k, half].astype(F32)
    for k in order:
        second[k].wait_recv()
        total = keep_buf[k] + twin_buf[k].astype(F32)
        if k:
            sum_buf[k] = total.astype(BF16)
            third[k] = send(sum_buf.at[k], wide_buf.at[k], send2.at[k], recv2.at[k], {"wide": peer(k)})
    for k in range(1, chips):
        third[k].wait_recv()
        total = total + wide_buf[k].astype(F32)
    narrow_buf[mine] = total.astype(BF16)
    slot = narrow_buf.at[mine]
    fourth = [send(slot, slot, send3.at[j], recv3.at[j], other) for j, other in enumerate(others)]
    for copy in fourth:
        copy.wait_recv()
    lanes = total.shape[1]
    for h in range(2):
        result = narrow_buf[h].astype(F32)
        for j in range(h + 2, copies_of, 2):
            result = result + narrow_buf[j].astype(F32)
        out_ref[:, h * lanes : (h + 1) * lanes] = result
    for copy in list(first.values()) + list(second.values()) + list(third.values()) + fourth:
        copy.wait_send()


def reduce_shares(packed, n, copies_of):
    chips = n // 2
    rows, lanes = packed.shape[2:]
    sems = pltpu.SemaphoreType.DMA((chips,))
    few = pltpu.SemaphoreType.DMA((copies_of,))
    part = lambda kind: pltpu.VMEM((chips, rows, lanes), kind)
    return pl.pallas_call(
        functools.partial(reduce_kernel, n, copies_of),
        out_shape=jax.ShapeDtypeStruct((rows, 2 * lanes), F32),
        in_specs=[pl.BlockSpec(memory_space=pl.ANY)],
        out_specs=pl.BlockSpec(memory_space=pltpu.VMEM),
        scratch_shapes=[pltpu.VMEM(packed.shape, BF16), pltpu.VMEM((chips, 2, rows, lanes), BF16), part(F32),
                        part(BF16), part(BF16), part(BF16), part(BF16), pltpu.VMEM((copies_of, rows, lanes), BF16),
                        pltpu.SemaphoreType.DMA] + [sems] * 6 + [few] * 2,
        compiler_params=pltpu.CompilerParams(collective_id=1, has_side_effects=True, vmem_limit_bytes=56000000),
        name="reduce",
    )(packed)


def adamw(weight, first_m, second_m, grad, decay):
    new_m = 0.9 * first_m + 0.1 * grad
    new_v = 0.999 * second_m + 0.001 * grad * grad
    ratio = new_m / (1.0 - 0.9**STEP) / (jnp.sqrt(new_v / (1.0 - 0.999**STEP)) + 1e-08)
    return (weight - 0.1 * (ratio + decay * weight), new_m, new_v)


def update_kernel(grad_ref, *refs):
    ins, outs = refs[:12], refs[12:]
    width = ins[0].shape[2]
    depth = ins[0].shape[0]
    extra = ins[6].shape[0] // 4

    def step(base, index, grad, decay):
        for ref, value in zip(outs[base : base + 3], adamw(*(r[index] for r in ins[base : base + 3]), grad, decay)):
            ref[index] = value

    for i in range(4):
        step(0, (slice(None), i, slice(None)), grad_ref[:depth, i * width : (i + 1) * width], 0.01)
    step(3, (slice(None), slice(None)), grad_ref[:depth, 4 * width :], 0.01)
    for j in range(4):
        step(6, (slice(j * extra, (j + 1) * extra), slice(None)), grad_ref[depth:, j * width : (j + 1) * width], 0.01)
    per_vec = ins[9].shape[1]
    step(9, (slice(None), slice(None)), grad_ref[depth : depth + 1, 4 * width : 4 * width + per_vec], 0.0)


def update(grad, states):
    vmem = pl.BlockSpec(memory_space=pltpu.VMEM)
    return pl.pallas_call(
        update_kernel,
        out_shape=[jax.ShapeDtypeStruct(a.shape, F32) for a in states],
        in_specs=[vmem] * 13,
        out_specs=[vmem] * 12,
        compiler_params=pltpu.CompilerParams(vmem_limit_bytes=4 * 1024 * 1024),
        name="update",
    )(grad, *states)


def on_device(layer_input, mask, dout, attn_w, ffn_in, ffn_out, vec,
              m_attn, v_attn, m_in, v_in, m_out, v_out, m_vec, v_vec):
    n, copies_of = lax.axis_size("wide"), lax.axis_size("narrow")
    turn = lambda a: a.transpose(1, 0, 2)
    row = lambda a: a.reshape(1, -1)
    full = gather(turn(attn_w), ffn_in, ffn_out, row(vec), n, copies_of)
    y, dx, packed = run_layer(layer_input.transpose(0, 2, 1), mask, dout.transpose(0, 2, 1), full, GROUP)
    share = reduce_shares(packed, n, copies_of)
    new = update(share, [turn(attn_w), turn(m_attn), turn(v_attn), ffn_in, m_in, v_in, ffn_out, m_out, v_out,
                         row(vec), row(m_vec), row(v_vec)])
    return (y.transpose(0, 2, 1), dx.transpose(0, 2, 1), *(turn(a) for a in new[:3]), *new[3:9],
            *(a.reshape(-1) for a in new[9:]))


def solution(mesh):
    rows = P(("wide", "narrow"), None, None)
    states = [P(None, "wide", None), P("wide", None), P("wide", None), P("wide")]
    moments = [s for s in states for _ in range(2)]
    results = [s for s in states for _ in range(3)]
    return jax.shard_map(
        on_device,
        mesh=mesh,
        in_specs=tuple([rows, P(("wide", "narrow"), None), rows] + states + moments),
        out_specs=tuple([rows, rows] + results),
        check_vma=False,
    )
```

```python
import functools
import jax
import jax.numpy as jnp
from jax import lax
from jax.experimental import pallas as pl
from jax.experimental.pallas import tpu as pltpu
from jax.sharding import PartitionSpec as P

H = 8
FH = 256
STEP = 10
LANES = 128
FORWARD = (0, 1, 7, 8, 9, 12)
BACKWARD = (0, 0, 1, 4, 5, 8)
GROUP = 16
F32 = jnp.float32
BF16 = jnp.bfloat16
NN = (((1,), (0,)), ((), ()))
NT = (((1,), (1,)), ((), ()))


def mm(a, b, dims=NN):
    return lax.dot_general(a, b, dims, preferred_element_type=F32)


def layer_kernel(
    group,
    x_hbm, mask_hbm, g_hbm, full_hbm,
    y_hbm, dx_hbm, packed_ref,
    big, w2f, vec_s, wqkv_ref, wo_ref, w1_ref, w2_ref,
    wqkvt, wot, w1t, w2t, cols, n1a, n2a, oa, ha, e_s,
    gqkv_ref, go_ref, g1_ref, g2_ref, ln_acc, pack_s, gqkvt_ref, g1t_ref,
    q_s, k_s, v_s, d_s, c_s, dqkv_s, o_s, inv_s, et_s,
    full_ref, mask_ref, x_b, g_b, y_b, dx_b, once_sem, in_sem, out_sem,
):
    step = pl.program_id(0)
    length = x_hbm.shape[2]
    width = x_hbm.shape[1]
    slot = lax.rem(step, 2)
    steps = x_hbm.shape[0] // group
    x_ref, g_ref, y_ref, dx_ref = (b.at[slot] for b in (x_b, g_b, y_b, dx_b))

    def arriving(index):
        into = lax.rem(index, 2)
        rows = pl.ds(index * group, group)
        return [
            pltpu.make_async_copy(x_hbm.at[rows], x_b.at[into], in_sem.at[0, into]),
            pltpu.make_async_copy(g_hbm.at[rows], g_b.at[into], in_sem.at[1, into]),
        ]

    def leaving(index):
        out_of = lax.rem(index, 2)
        rows = pl.ds(index * group, group)
        return [
            pltpu.make_async_copy(y_b.at[out_of], y_hbm.at[rows], out_sem.at[0, out_of]),
            pltpu.make_async_copy(dx_b.at[out_of], dx_hbm.at[rows], out_sem.at[1, out_of]),
        ]
    head = width // H
    tokens = group * LANES
    factor = float(head) ** (-0.5)
    log2e = 1.4426950408889634

    @pl.when(step == 0)
    def _():
        first = [
            pltpu.make_async_copy(full_hbm, full_ref, once_sem.at[0]),
            pltpu.make_async_copy(mask_hbm, mask_ref, once_sem.at[1]),
        ]
        for copy in first + arriving(0):
            copy.start()
        for copy in first:
            copy.wait()
        shards, _, block_rows, _ = full_ref.shape
        depth = width // shards
        extra = block_rows - depth
        per_vec = vec_s.shape[1] // shards
        for w in range(shards):
            block = jnp.concatenate([full_ref[w, 0], full_ref[w, 1]], axis=1).astype(F32)
            big[w * depth : (w + 1) * depth, :] = block[:depth]
            for j in range(4):
                at = (4 * w + j) * extra
                w2f[at : at + extra, :] = block[depth:, j * width : (j + 1) * width]
            vec_s[:, w * per_vec : (w + 1) * per_vec] = block[depth : depth + 1, 4 * width : 4 * width + per_vec]
        wqkv_ref[...] = big[:, : 3 * width].astype(BF16)
        wo_ref[...] = big[:, 3 * width : 4 * width].astype(BF16)
        w1_ref[...] = big[:, 4 * width :].astype(BF16)
        w2_ref[...] = w2f[...].astype(BF16)

        def aug(w, bias):
            rows = lax.broadcasted_iota(jnp.int32, (64, w.shape[1]), 0)
            tail = jnp.where(rows == 0, jnp.broadcast_to(bias, (64, w.shape[1])), 0.0)
            return jnp.concatenate([w.astype(F32), tail], axis=0).T.astype(BF16)

        zero_row = jnp.zeros((1, width), F32)
        v = vec_s[...]
        piece = lambda i: v[:, i * width : (i + 1) * width]
        bias_qkv = jnp.concatenate([piece(2), zero_row, piece(3)], axis=1)
        wqkvt[...] = aug(wqkv_ref[...], bias_qkv)
        wot[...] = aug(wo_ref[...], piece(4))
        w1t[...] = aug(w1_ref[...], v[:, 8 * width : 8 * width + 2 * FH])
        w2t[...] = w2_ref[...].astype(F32).T.astype(BF16)
        for j, i in enumerate((0, 1, 5, 6, 7)):
            cols[j] = jnp.broadcast_to(piece(i), (LANES, width)).T
        rows = lax.broadcasted_iota(jnp.int32, (64, tokens), 0)
        one = jnp.where(rows == 0, 1.0, 0.0).astype(BF16)
        n1a[width:, :] = one
        n2a[width:, :] = one
        oa[width:, :] = one
        ha[FH:, :] = one[:16]
        gqkvt_ref[...] = jnp.zeros_like(gqkvt_ref)
        go_ref[...] = jnp.zeros_like(go_ref)
        g1t_ref[...] = jnp.zeros_like(g1t_ref)
        g2_ref[...] = jnp.zeros_like(g2_ref)
        ln_acc[...] = jnp.zeros_like(ln_acc)
        pack_s[...] = jnp.zeros_like(pack_s)

    @pl.when(step + 1 < pl.num_programs(0))
    def _():
        for copy in arriving(step + 1):
            copy.start()

    for copy in arriving(step):
        copy.wait()

    @pl.when(step > 1)
    def _():
        for copy in leaving(step - 2):
            copy.wait()

    def wide(ref, g):
        t = ref[g]
        return jnp.concatenate([t, jnp.zeros((width, LANES - length), t.dtype)], axis=1)

    def tile(col):
        return jnp.concatenate([col] * group, axis=1) if group > 1 else col

    def norm(value):
        center = value - jnp.sum(value, 0, keepdims=True) * (1.0 / width)
        rstd = lax.rsqrt(jnp.sum(center * center, 0, keepdims=True) * (1.0 / width) + 1e-05)
        return center * rstd, rstd

    def norm_back(dn, xhat, rstd, gain, which):
        prod = dn * xhat
        total = ln_acc[which]
        for g in range(dn.shape[1] // LANES):
            total = total + prod[:, g * LANES : (g + 1) * LANES]
        ln_acc[which] = total
        t = dn * gain
        m1 = jnp.sum(t, 0, keepdims=True) * (1.0 / width)
        m2 = jnp.sum(t * xhat, 0, keepdims=True) * (1.0 / width)
        return rstd * (t - m1 - xhat * m2)

    gain1, bias1, gain2, bias2, bias_c2 = (tile(cols[j]) for j in range(5))

    x = jnp.concatenate([wide(x_ref, g) for g in range(group)], axis=1).astype(F32)
    xhat1, rstd1 = norm(x)
    n1a[:width, :] = (xhat1 * gain1 + bias1).astype(BF16)
    qkv = mm(wqkvt[...], n1a[...])

    sub = lax.broadcasted_iota(jnp.int32, (16, LANES), 0)
    lane = lax.broadcasted_iota(jnp.int32, (16, LANES), 1)
    ones_q = jnp.where(sub == 0, 1.0, 0.0)
    ones_v = jnp.where(sub < 2, 1.0, 0.0)
    empty = jnp.zeros((head, LANES), F32)
    two = 2 * head
    live = {}

    def block_diag(first, second, tail_first, tail_second):
        left = jnp.concatenate([first, empty, tail_first], axis=0).astype(BF16)
        right = jnp.concatenate([empty, second, tail_second], axis=0).astype(BF16)
        return jnp.concatenate([left, right], axis=1)

    def run(stages, lags):
        items = [(g, p) for g in range(group) for p in range(H // 2)]
        for t in range(len(items) + max(lags)):
            for stage, lag in reversed(list(zip(stages, lags))):
                if 0 <= t - lag < len(items):
                    stage(t - lag, *items[t - lag])

    def forward_prepare(t, g, p):
        sl = slice(g * LANES, (g + 1) * LANES)
        m = mask_ref[pl.ds(step * group + g, 1), :]
        m = jnp.concatenate([m, jnp.zeros((1, LANES - length), jnp.int32)], axis=1)
        ok = (jnp.broadcast_to(m, (16, LANES)) != 0) | (lane == 0)
        tail_k = jnp.where((sub == 0) & jnp.logical_not(ok), -1e30, 0.0)
        lo = p * two
        q_s[g, p] = block_diag(qkv[lo : lo + head, sl], qkv[lo + head : lo + two, sl], ones_q, ones_q)
        kp = jnp.concatenate([qkv[width + lo : width + lo + two, sl], tail_k], axis=0).astype(BF16)
        k_s[g, p] = kp
        v_s[g, p] = jnp.concatenate([qkv[2 * width + lo : 2 * width + lo + two, sl], ones_v], axis=0).astype(BF16)
        live["k", t] = kp.T

    def forward_scores(t, g, p):
        live["s", t] = mm(live.pop(("k", t)), q_s[g, p])

    def forward_top(t, g, p):
        live["m", t] = jnp.max(live["s", t], 0, keepdims=True)

    def forward_exp(t, g, p):
        e_s[g, p] = jnp.exp2((live.pop(("s", t)) - live.pop(("m", t))) * (factor * log2e)).astype(BF16)

    def forward_mix(t, g, p):
        live["n", t] = mm(v_s[g, p], e_s[g, p])

    def forward_out(t, g, p):
        num = live.pop(("n", t))
        inv = 1.0 / num[two : two + 1]
        inv_s[g, p : p + 1, :] = inv
        sl = slice(g * LANES, (g + 1) * LANES)
        lo = p * two
        o_s[lo : lo + head, sl] = num[:head, :LANES] * inv[:, :LANES]
        o_s[lo + head : lo + two, sl] = num[head:two, LANES:] * inv[:, LANES:]

    run([forward_prepare, forward_scores, forward_top, forward_exp, forward_mix, forward_out], FORWARD)
    oa[:width, :] = o_s[...].astype(BF16)
    x1 = x + mm(wot[...], oa[...])
    xhat2, rstd2 = norm(x1)
    n2a[:width, :] = (xhat2 * gain2 + bias2).astype(BF16)
    gt = jnp.concatenate([wide(g_ref, g) for g in range(group)], axis=1)
    dz_tiles = []
    for t in range(tokens // 256):
        sl = slice(t * 256, (t + 1) * 256)
        z = mm(w1t[...], n2a[:, sl])
        dh = mm(w2_ref[...], gt[:, sl])
        das, dbs = [], []
        for c in range(FH // 64):
            part_a, part_b = z[c * 64 : (c + 1) * 64], z[FH + c * 64 : FH + (c + 1) * 64]
            grad = dh[c * 64 : (c + 1) * 64]
            sigm = 1.0 / (1.0 + jnp.exp2(part_b * -log2e))
            silu = part_b * sigm
            ha[c * 64 : (c + 1) * 64, sl] = (part_a * silu).astype(BF16)
            das.append((grad * silu).astype(BF16))
            dbs.append((grad * part_a * (sigm + silu * (1.0 - sigm))).astype(BF16))
        dz_tiles.append(jnp.concatenate(das + dbs, axis=0))
    dz = jnp.concatenate(dz_tiles, axis=1)
    g2_ref[...] += mm(ha[...], gt, NT)
    g1t_ref[...] += mm(dz, n2a[:208, :], NT)
    dn2 = mm(w1_ref[...], dz)
    dx1 = gt.astype(F32) + norm_back(dn2, xhat2, rstd2, gain2, 1)
    da1 = dx1.astype(BF16)
    go_ref[...] += mm(oa[:208, :], da1, NT)
    do = mm(wo_ref[...], da1).astype(BF16).astype(F32)
    y = (x1 + mm(w2t[...], ha[:FH, :]) + bias_c2).astype(BF16)
    for g in range(group):
        y_ref[g] = y[:, g * LANES : g * LANES + length]

    def backward_prepare(t, g, p):
        sl = slice(g * LANES, (g + 1) * LANES)
        rows, tails = [], []
        for j in range(2):
            r = slice(p * two + j * head, p * two + (j + 1) * head)
            d = do[r, sl]
            inv = inv_s[g, p : p + 1, j * LANES : (j + 1) * LANES]
            low = jnp.sum(d * o_s[r, sl], 0, keepdims=True) * -inv
            hi = low.astype(BF16).astype(F32)
            rows.append(d * inv)
            tails.append(jnp.where(sub == 0, hi, jnp.where(sub == 1, low - hi, 0.0)))
        d_s[g, p] = block_diag(*rows, *tails)
        live["v", t] = v_s[g, p].T
        live["r", t] = jnp.concatenate(rows, axis=0).astype(BF16)

    def backward_probs(t, g, p):
        live["p", t] = mm(live.pop(("v", t)), d_s[g, p])

    def backward_scores(t, g, p):
        c_s[g, p] = (e_s[g, p].astype(F32) * live.pop(("p", t))).astype(BF16)

    def backward_turn(t, g, p):
        e = e_s[g, p]
        et_s[g, p] = jnp.concatenate([e[:, :LANES].T, e[:, LANES:].T], axis=1)

    def backward_mix(t, g, p):
        live["dv", t] = mm(live.pop(("r", t)), et_s[g, p])
        live["dk", t] = mm(q_s[g, p, :two], c_s[g, p], NT)
        live["dq", t] = mm(k_s[g, p, :two], c_s[g, p])

    def backward_out(t, g, p):
        sl = slice(g * LANES, (g + 1) * LANES)
        lo = p * two
        dq = live.pop(("dq", t))
        dq = jnp.concatenate([dq[:head, :LANES], dq[head:, LANES:]], axis=0)
        dqkv_s[lo : lo + two, sl] = (dq * factor).astype(BF16)
        dqkv_s[width + lo : width + lo + two, sl] = (live.pop(("dk", t)) * factor).astype(BF16)
        dv = live.pop(("dv", t))
        dv = jnp.concatenate([dv[:head, :LANES], dv[head:, LANES:]], axis=0)
        dqkv_s[2 * width + lo : 2 * width + lo + two, sl] = dv.astype(BF16)

    run([backward_prepare, backward_turn, backward_probs, backward_scores, backward_mix, backward_out], BACKWARD)
    dqkv = dqkv_s[...]
    gqkvt_ref[...] += mm(dqkv, n1a[:208, :], NT)
    dn1 = mm(wqkv_ref[...], dqkv)
    dx = (dx1 + norm_back(dn1, xhat1, rstd1, gain1, 0)).astype(BF16)
    for g in range(group):
        dx_ref[g] = dx[:, g * LANES : g * LANES + length]

    for copy in leaving(step):
        copy.start()

    @pl.when(step == pl.num_programs(0) - 1)
    def _():
        gqkv_ref[...] = gqkvt_ref[...].T
        g1_ref[...] = g1t_ref[...].T
        gains = [jnp.sum(ln_acc[i].T, 0, keepdims=True) for i in range(2)]

        def through(weights, sums):
            return jnp.sum(weights[:, :width].astype(F32) * sums[:, width : width + 1], 0, keepdims=True)

        rows = [gains[0], through(wqkvt, gqkvt_ref), gains[1], through(w1t, g1t_ref)]
        vec = jnp.concatenate(
            [rows[0], rows[1], gqkv_ref[width : width + 1, :width], gqkv_ref[width : width + 1, 2 * width :],
             go_ref[width : width + 1], rows[2], rows[3], g2_ref[FH : FH + 1], g1_ref[width : width + 1]],
            axis=1,
        )
        shards, _, block_rows, half = packed_ref.shape
        depth = width // shards
        extra = block_rows - depth
        per_vec = vec.shape[1] // shards
        for w in range(shards):
            r = slice(w * depth, (w + 1) * depth)
            pack_s[w, :depth, : 4 * width] = jnp.concatenate([gqkv_ref[r, :], go_ref[r, :]], axis=1)
            pack_s[w, :depth, 4 * width :] = g1_ref[r, :]
            at = 4 * w * extra
            pack_s[w, depth:, : 4 * width] = jnp.concatenate(
                [g2_ref[at + j * extra : at + (j + 1) * extra, :] for j in range(4)], axis=1
            )
            pack_s[w, depth : depth + 1, 4 * width : 4 * width + per_vec] = vec[:, w * per_vec : (w + 1) * per_vec]
        for j in range(2):
            packed_ref[:, j] = pack_s[:, :, j * half : (j + 1) * half].astype(BF16)
        for copy in leaving(step) + (leaving(step - 1) if steps > 1 else []):
            copy.wait()


def run_layer(x, mask, dout, full, group):
    samples, width, length = x.shape
    tokens = group * LANES
    whole = lambda a: pl.BlockSpec(a.shape, lambda i: (0,) * a.ndim)
    apart = pl.BlockSpec(memory_space=pl.ANY)
    block = (group, width, length)
    return pl.pallas_call(
        functools.partial(layer_kernel, group),
        grid=(samples // group,),
        in_specs=[apart] * 4,
        out_specs=[apart, apart, whole(full)],
        out_shape=[jax.ShapeDtypeStruct(x.shape, BF16)] * 2 + [jax.ShapeDtypeStruct(full.shape, BF16)],
        scratch_shapes=[
            pltpu.VMEM((width, 4 * width + 2 * FH), F32),
            pltpu.VMEM((FH, width), F32),
            pltpu.VMEM((1, 8 * width + 2 * FH), F32),
            pltpu.VMEM((width, 3 * width), BF16),
            pltpu.VMEM((width, width), BF16),
            pltpu.VMEM((width, 2 * FH), BF16),
            pltpu.VMEM((FH, width), BF16),
            pltpu.VMEM((3 * width, 256), BF16),
            pltpu.VMEM((width, 256), BF16),
            pltpu.VMEM((2 * FH, 256), BF16),
            pltpu.VMEM((width, FH), BF16),
            pltpu.VMEM((5, width, LANES), F32),
            pltpu.VMEM((256, tokens), BF16),
            pltpu.VMEM((256, tokens), BF16),
            pltpu.VMEM((256, tokens), BF16),
            pltpu.VMEM((272, tokens), BF16),
            pltpu.VMEM((group, H // 2, LANES, 2 * LANES), BF16),
            pltpu.VMEM((208, 3 * width), F32),
            pltpu.VMEM((208, width), F32),
            pltpu.VMEM((208, 2 * FH), F32),
            pltpu.VMEM((272, width), F32),
            pltpu.VMEM((2, width, LANES), F32),
            pltpu.VMEM((full.shape[0], full.shape[2], 2 * full.shape[3]), F32),
            pltpu.VMEM((3 * width, 208), F32),
            pltpu.VMEM((2 * FH, 208), F32),
            pltpu.VMEM((group, H // 2, 64, 2 * LANES), BF16),
            pltpu.VMEM((group, H // 2, 64, LANES), BF16),
            pltpu.VMEM((group, H // 2, 64, LANES), BF16),
            pltpu.VMEM((group, H // 2, 64, 2 * LANES), BF16),
            pltpu.VMEM((group, H // 2, LANES, 2 * LANES), BF16),
            pltpu.VMEM((3 * width, tokens), BF16),
            pltpu.VMEM((width, tokens), F32),
            pltpu.VMEM((group, H // 2, 2 * LANES), F32),
            pltpu.VMEM((group, H // 2, LANES, 2 * LANES), BF16),
            pltpu.VMEM(full.shape, BF16),
            pltpu.VMEM(mask.shape, jnp.int32),
            pltpu.VMEM((2,) + block, BF16),
            pltpu.VMEM((2,) + block, BF16),
            pltpu.VMEM((2,) + block, BF16),
            pltpu.VMEM((2,) + block, BF16),
            pltpu.SemaphoreType.DMA((2,)),
            pltpu.SemaphoreType.DMA((2, 2)),
            pltpu.SemaphoreType.DMA((2, 2)),
        ],
        compiler_params=pltpu.CompilerParams(vmem_limit_bytes=60 * 1024 * 1024),
        name="layer",
    )(x, mask, dout, full)


def send(src, dst, send_sem, recv_sem, device):
    copy = pltpu.make_async_remote_copy(
        src_ref=src, dst_ref=dst, send_sem=send_sem, recv_sem=recv_sem,
        device_id=device, device_id_type=pl.DeviceIdType.MESH,
    )
    copy.start()
    return copy


def hail(devices):
    barrier = pltpu.get_barrier_semaphore()
    for device in devices:
        pl.semaphore_signal(barrier, inc=1, device_id=device, device_id_type=pl.DeviceIdType.MESH)


def places(n, copies_of):
    me, mine = lax.axis_index("wide"), lax.axis_index("narrow")
    core, chip, chips = lax.rem(me, 2), lax.div(me, 2), n // 2
    peer = lambda k: 2 * lax.bitwise_xor(chip, k) + core
    half = lax.rem(mine, 2)
    sibling = {"wide": me + 1 - 2 * core}
    twin = {"narrow": mine + 1 - 2 * half}
    return me, mine, core, chips, peer, half, sibling, twin


def gather_kernel(n, copies_of, attn_hbm, w1_hbm, w2_hbm, vec_hbm, out_ref, attn_ref, w1_ref, w2_ref, vec_ref, load,
                  send1, recv1, send2, recv2, send3, recv3, send4, recv4):
    me, mine, core, chips, peer, half, sibling, twin = places(n, copies_of)
    met = [{"wide": peer(k)} for k in range(1, chips)] + [sibling, twin]
    hail(met)
    pairs = ((attn_hbm, attn_ref), (w1_hbm, w1_ref), (w2_hbm, w2_ref), (vec_hbm, vec_ref))
    loads = [pltpu.make_async_copy(a, b, load.at[i]) for i, (a, b) in enumerate(pairs)]
    for copy in loads:
        copy.start()
    for copy in loads:
        copy.wait()
    width = attn_ref.shape[2]
    extra = w2_ref.shape[0] // 4
    lanes = out_ref.shape[3]
    top = jnp.concatenate([attn_ref[:, i, :] for i in range(4)] + [w1_ref[...]], axis=1)
    bottom = jnp.concatenate(
        [w2_ref[j * extra : (j + 1) * extra, :] for j in range(4)]
        + [jnp.broadcast_to(vec_ref[...], (extra, vec_ref.shape[1])),
           jnp.zeros((extra, 2 * lanes - 4 * width - vec_ref.shape[1]), F32)],
        axis=1,
    )
    block = jnp.concatenate([top, bottom], axis=0).astype(BF16)
    out_ref[me, 0] = block[:, :lanes]
    out_ref[me, 1] = block[:, lanes:]
    pl.semaphore_wait(pltpu.get_barrier_semaphore(), len(met))
    whole, own = out_ref.at[me], out_ref.at[me, half]
    far, near = range(chips // 2, chips), range(1, chips // 2)
    copies = {}
    for k in far:
        copies[k] = send(own, own, send1.at[k], recv1.at[k], {"wide": peer(k)})
    for k in near:
        copies[k] = send(whole, whole, send1.at[k], recv1.at[k], {"wide": peer(k)})
    passed = [send(whole, whole, send2.at[0], recv2.at[0], sibling)]
    crossed = {}
    for k in near:
        copies[k].wait_recv()
        got = out_ref.at[peer(k)]
        passed.append(send(got, got, send2.at[k], recv2.at[k], sibling))
    for k in far:
        copies[k].wait_recv()
        got = out_ref.at[peer(k), half]
        crossed[k] = send(got, got, send3.at[k], recv3.at[k], twin)
        passed.append(send(got, got, send2.at[k], recv2.at[k], sibling))
    for k in far:
        crossed[k].wait_recv()
        got = out_ref.at[peer(k), 1 - half]
        passed.append(send(got, got, send4.at[k], recv4.at[k], sibling))
    for copy in list(copies.values()) + list(crossed.values()):
        copy.wait_send()
    for copy in passed:
        copy.wait()


def gather(attn, w1, w2, vec, n, copies_of):
    rows = attn.shape[0] + w2.shape[0] // 4
    lanes = 4 * attn.shape[2] + w1.shape[1]
    sems = pltpu.SemaphoreType.DMA((n // 2,))
    return pl.pallas_call(
        functools.partial(gather_kernel, n, copies_of),
        out_shape=jax.ShapeDtypeStruct((n, 2, rows, lanes // 2), BF16),
        in_specs=[pl.BlockSpec(memory_space=pl.ANY)] * 4,
        out_specs=pl.BlockSpec(memory_space=pltpu.VMEM),
        scratch_shapes=[pltpu.VMEM(a.shape, F32) for a in (attn, w1, w2, vec)]
        + [pltpu.SemaphoreType.DMA((4,))] + [sems] * 8,
        compiler_params=pltpu.CompilerParams(collective_id=0, has_side_effects=True),
        name="gather",
    )(attn, w1, w2, vec)


def reduce_kernel(n, copies_of, part_hbm, out_ref, part_ref, core_buf, keep_buf, turn_buf, twin_buf, sum_buf,
                  far_buf, near_out, near_buf, late_out, late_buf, narrow_buf, load,
                  send0, recv0, send1, recv1, send2, recv2, send3, recv3, send4, recv4, late_sem):
    me, mine, core, chips, peer, half, sibling, twin = places(n, copies_of)
    others = [{"narrow": lax.rem(mine + j, copies_of)} for j in range(1, copies_of)]
    met = [{"wide": peer(k)} for k in range(1, chips)] + [sibling] + others
    hail(met)
    mine_parts = pltpu.make_async_copy(part_hbm, part_ref, load)
    mine_parts.start()
    mine_parts.wait()
    pl.semaphore_wait(pltpu.get_barrier_semaphore(), len(met))
    far = list(reversed(range(chips // 2, chips)))
    near = list(reversed(range(1, chips // 2)))
    first, second, third, direct = {}, {}, {}, {}
    for k in far + near + [0]:
        first[k] = send(part_ref.at[peer(k) + 1 - 2 * core], core_buf.at[k], send0.at[k], recv0.at[k], sibling)

    def chip_sum(k, h):
        return part_ref[peer(k), h].astype(F32) + core_buf[k, h].astype(F32)

    for k in far:
        first[k].wait_recv()
        turn_buf[k] = chip_sum(k, 1 - half).astype(BF16)
        second[k] = send(turn_buf.at[k], twin_buf.at[k], send1.at[k], recv1.at[k], twin)
        keep_buf[k] = chip_sum(k, half)
    for k in near:
        first[k].wait_recv()
        for h in range(2):
            near_out[k, h] = chip_sum(k, h).astype(BF16)
        direct[k] = send(near_out.at[k], near_buf.at[k], send2.at[k], recv2.at[k], {"wide": peer(k)})
    first[0].wait_recv()
    for k in far:
        second[k].wait_recv()
        sum_buf[k] = (keep_buf[k] + twin_buf[k].astype(F32)).astype(BF16)
        third[k] = send(sum_buf.at[k], far_buf.at[k], send3.at[k], recv3.at[k], {"wide": peer(k)})
    total, across = chip_sum(0, half), chip_sum(0, 1 - half)
    for k in near:
        direct[k].wait_recv()
        total = total + near_buf[k, half].astype(F32)
        across = across + near_buf[k, 1 - half].astype(F32)
    late_out[...] = across.astype(BF16)
    late = send(late_out, late_buf, late_sem.at[0], late_sem.at[1], twin)
    for k in far:
        third[k].wait_recv()
        total = total + far_buf[k].astype(F32)
    late.wait_recv()
    total = total + late_buf[...].astype(F32)
    narrow_buf[mine] = total.astype(BF16)
    slot = narrow_buf.at[mine]
    fourth = [send(slot, slot, send4.at[j], recv4.at[j], other) for j, other in enumerate(others)]
    for copy in fourth:
        copy.wait_recv()
    lanes = total.shape[1]
    for h in range(2):
        result = narrow_buf[h].astype(F32)
        for j in range(h + 2, copies_of, 2):
            result = result + narrow_buf[j].astype(F32)
        out_ref[:, h * lanes : (h + 1) * lanes] = result
    for group_of in (first, second, third, direct):
        for copy in group_of.values():
            copy.wait_send()
    for copy in [late] + fourth:
        copy.wait_send()


def reduce_shares(packed, n, copies_of):
    chips = n // 2
    rows, lanes = packed.shape[2:]
    sems = pltpu.SemaphoreType.DMA((chips,))
    few = pltpu.SemaphoreType.DMA((copies_of,))
    part = lambda kind: pltpu.VMEM((chips, rows, lanes), kind)
    pair = pltpu.VMEM((chips, 2, rows, lanes), BF16)
    one = pltpu.VMEM((rows, lanes), BF16)
    return pl.pallas_call(
        functools.partial(reduce_kernel, n, copies_of),
        out_shape=jax.ShapeDtypeStruct((rows, 2 * lanes), F32),
        in_specs=[pl.BlockSpec(memory_space=pl.ANY)],
        out_specs=pl.BlockSpec(memory_space=pltpu.VMEM),
        scratch_shapes=[pltpu.VMEM(packed.shape, BF16), pair, part(F32), part(BF16), part(BF16), part(BF16),
                        part(BF16), pair, pair, one, one, pltpu.VMEM((copies_of, rows, lanes), BF16),
                        pltpu.SemaphoreType.DMA] + [sems] * 8 + [few] * 2 + [pltpu.SemaphoreType.DMA((2,))],
        compiler_params=pltpu.CompilerParams(collective_id=1, has_side_effects=True, vmem_limit_bytes=56000000),
        name="reduce",
    )(packed)


def adamw(weight, first_m, second_m, grad, decay):
    new_m = 0.9 * first_m + 0.1 * grad
    new_v = 0.999 * second_m + 0.001 * grad * grad
    ratio = new_m / (1.0 - 0.9**STEP) / (jnp.sqrt(new_v / (1.0 - 0.999**STEP)) + 1e-08)
    return (weight - 0.1 * (ratio + decay * weight), new_m, new_v)


def update_kernel(grad_ref, *refs):
    ins, outs = refs[:12], refs[12:]
    width = ins[0].shape[2]
    depth = ins[0].shape[0]
    extra = ins[6].shape[0] // 4

    def step(base, index, grad, decay):
        for ref, value in zip(outs[base : base + 3], adamw(*(r[index] for r in ins[base : base + 3]), grad, decay)):
            ref[index] = value

    for i in range(4):
        step(0, (slice(None), i, slice(None)), grad_ref[:depth, i * width : (i + 1) * width], 0.01)
    step(3, (slice(None), slice(None)), grad_ref[:depth, 4 * width :], 0.01)
    for j in range(4):
        step(6, (slice(j * extra, (j + 1) * extra), slice(None)), grad_ref[depth:, j * width : (j + 1) * width], 0.01)
    per_vec = ins[9].shape[1]
    step(9, (slice(None), slice(None)), grad_ref[depth : depth + 1, 4 * width : 4 * width + per_vec], 0.0)


def update(grad, states):
    vmem = pl.BlockSpec(memory_space=pltpu.VMEM)
    return pl.pallas_call(
        update_kernel,
        out_shape=[jax.ShapeDtypeStruct(a.shape, F32) for a in states],
        in_specs=[vmem] * 13,
        out_specs=[vmem] * 12,
        compiler_params=pltpu.CompilerParams(vmem_limit_bytes=4 * 1024 * 1024),
        name="update",
    )(grad, *states)


def on_device(layer_input, mask, dout, attn_w, ffn_in, ffn_out, vec,
              m_attn, v_attn, m_in, v_in, m_out, v_out, m_vec, v_vec):
    n, copies_of = lax.axis_size("wide"), lax.axis_size("narrow")
    turn = lambda a: a.transpose(1, 0, 2)
    row = lambda a: a.reshape(1, -1)
    full = gather(turn(attn_w), ffn_in, ffn_out, row(vec), n, copies_of)
    y, dx, packed = run_layer(layer_input.transpose(0, 2, 1), mask, dout.transpose(0, 2, 1), full, GROUP)
    share = reduce_shares(packed, n, copies_of)
    new = update(share, [turn(attn_w), turn(m_attn), turn(v_attn), ffn_in, m_in, v_in, ffn_out, m_out, v_out,
                         row(vec), row(m_vec), row(v_vec)])
    return (y.transpose(0, 2, 1), dx.transpose(0, 2, 1), *(turn(a) for a in new[:3]), *new[3:9],
            *(a.reshape(-1) for a in new[9:]))


def solution(mesh):
    rows = P(("wide", "narrow"), None, None)
    states = [P(None, "wide", None), P("wide", None), P("wide", None), P("wide")]
    moments = [s for s in states for _ in range(2)]
    results = [s for s in states for _ in range(3)]
    return jax.shard_map(
        on_device,
        mesh=mesh,
        in_specs=tuple([rows, P(("wide", "narrow"), None), rows] + states + moments),
        out_specs=tuple([rows, rows] + results),
        check_vma=False,
    )
```
